128 devices in a mesh: clip: 32 (over y, x, core), seq: 4 (over z).
Axes of the slice: x: 4, y: 4, z: 4, core: 2. Of those that a mesh axis runs over, the one named last changes fastest.
Arguments:
- vae_in: bfloat16 [512, 8, 32, 512], P('clip', 'seq'), may hold values from -6 to 6
- vae_gain: float32 [512], replicated, may hold values from 0.25 to 1.75
- w_conv: bfloat16 [3, 512, 512], replicated, may hold values from -0.15625 to 0.15625
- b_conv: float32 [512], replicated, may hold values from -3 to 3
- w_lat: bfloat16 [512, 16], replicated, may hold values from -0.25 to 0.25
- b_lat: float32 [16], replicated, may hold values from -3 to 3
- w_emb: bfloat16 [64, 3072], replicated, may hold values from -0.75 to 0.75
- b_emb: float32 [3072], replicated, may hold values from -3 to 3
- clip_lengths: int32 [64], replicated, may hold values from 6 to 8, as said below
- clip_owner: int32 [64], replicated, may hold values from 0 to 31
- clip_mod: float32 [64, 3, 3072], replicated, may hold values from -6 to 6
- w_qkv: bfloat16 [3072, 3, 3072], P(None, None, 'seq'), may hold values from -1 to 1
- w_out: bfloat16 [3072, 3072], P('seq'), may hold values from -0.109375 to 0.109375
Outputs:
- block_out: bfloat16 [512, 4, 16, 3072], P('clip', 'seq')
The draws below stay inside these ranges and needn't reach their ends.
Inputs may be any that keep to these rules, and one draw needn't show every extreme that they name: `clip_lengths`: clips lie end to end from frame 0 in index order; frames after the last clip belong to no clip. Clip r * 32 + p is owned by a group that depends on p alone, so every group owns 2 clips; the clips of the group at p = 0 have 8 frames each, so that group owns 16 frames. Among the 16 frames of one index of clip, at most 8 belong to one group, and on index 0 that many do.
All inputs are finite; a program needn't handle non-finite values.
Results may differ from the reference program's by a relative error of at most 0.015.
Values may be sent and summed in bfloat16 or wider, within the bound.
A program may use at most 192 MiB of HBM per device.

```python
import jax
import jax.numpy as jnp
from jax import lax

D = 3072
HEADS = 24
HD = 128
LAT = 16
CH = 512
WL = 32
CLIPS_G = 2
LEN_LO = 6
LEN_HI = 8
GROUPS = 32
CLIPS = 64
FRAMES = 512
HL = 8


def clip_plan(key):
    order = jax.random.permutation(jax.random.fold_in(key, 11), GROUPS).astype(jnp.int32)
    lengths = jax.random.randint(jax.random.fold_in(key, 12), (CLIPS_G, GROUPS), LEN_LO, LEN_HI + 1, dtype=jnp.int32)
    first = (jnp.arange(GROUPS, dtype=jnp.int32) == 0)[None, :]
    lengths = jnp.where(first, LEN_HI, lengths)
    owners = jnp.broadcast_to(order[None, :], (CLIPS_G, GROUPS))
    return (lengths.reshape(-1).astype(jnp.int32), owners.reshape(-1).astype(jnp.int32))


def draw_clip_lengths(key, part):
    lengths, owners = clip_plan(key)
    return lengths


def draw_clip_owner(key, part):
    lengths, owners = clip_plan(key)
    return owners


def draw_clip_mod(key, part):
    key = jax.random.fold_in(key, 31)
    keys = jax.random.split(key, 4)
    shift = 0.5 * jnp.clip(jax.random.normal(keys[2], (CLIPS, D), jnp.float32), -4.0, 4.0)
    scale = 0.25 * jnp.clip(jax.random.normal(keys[1], (CLIPS, D), jnp.float32), -4.0, 4.0)
    gate = jnp.clip(jax.random.normal(keys[3], (CLIPS, D), jnp.float32), -4.0, 4.0)
    return jnp.stack([shift, scale, gate], axis=1).astype(jnp.float32)


def draw_w_qkv(key, part):
    key = jax.random.fold_in(key, 41)
    keys = jax.random.split(key, 3)
    factor = D ** (-0.5)
    query = factor * jnp.clip(jax.random.normal(keys[0], (D, HEADS * HD), jnp.float32), -6.0, 6.0)
    other = factor * jnp.clip(jax.random.normal(keys[1], (D, HEADS * HD), jnp.float32), -6.0, 6.0)
    value = factor * jnp.clip(jax.random.normal(keys[2], (D, HEADS * HD), jnp.float32), -6.0, 6.0)
    keyed = other
    return jnp.stack([query, keyed, value], axis=1).astype(jnp.bfloat16)


def block_scale(key, shape, cuts, low, largest):
    def one(position, parts):
        steps = jax.random.uniform(jax.random.fold_in(jax.random.fold_in(key, 6), position), (parts,), jnp.float32, low / len(cuts), largest / len(cuts))
        return jnp.repeat(jnp.exp(steps), shape[position] // parts).reshape((-1,) + (1,) * (len(shape) - position - 1))

    factor_of = one(*cuts[0])
    for cut in cuts[1:]:
        factor_of = factor_of * one(*cut)
    return factor_of


def scatter_about(own_key, dims, scale, limit, pieces=(), kind=jnp.bfloat16):
    array = scale * jax.random.normal(own_key, dims, jnp.float32)
    if pieces:
        array = array * block_scale(own_key, dims, pieces, -0.22, 0.18)
    return jnp.clip(array, -limit, limit).astype(kind)


def setup_inputs(seed: int = 0) -> dict:
    key_of = jax.random.split(jax.random.key(seed), 14)
    vae_in = scatter_about(key_of[0], (FRAMES, HL, WL, CH), 1.0, 6.0, ((0, 32), (1, 4)))
    vae_gain = jnp.clip(1.0 + 0.15 * jax.random.normal(key_of[1], (CH,), jnp.float32), 0.25, 1.75)
    w_conv = scatter_about(key_of[2], (3, CH, CH), (3 * CH) ** -0.5, 0.15625)
    b_conv = scatter_about(key_of[3], (CH,), 0.5, 3.0, (), jnp.float32)
    w_lat = scatter_about(key_of[4], (CH, LAT), CH ** -0.5, 0.25)
    b_lat = scatter_about(key_of[5], (LAT,), 0.5, 3.0, (), jnp.float32)
    w_emb = scatter_about(key_of[6], (4 * LAT, D), (4 * LAT) ** -0.5, 0.75)
    b_emb = scatter_about(key_of[7], (D,), 0.5, 3.0, (), jnp.float32)
    clip_lengths = draw_clip_lengths(jax.random.fold_in(key_of[13], 71), 0)
    clip_owner = draw_clip_owner(jax.random.fold_in(key_of[13], 71), 0)
    clip_mod = draw_clip_mod(jax.random.fold_in(key_of[13], 71), 0)
    w_qkv = draw_w_qkv(jax.random.fold_in(key_of[13], 71), 0)
    w_out = scatter_about(key_of[12], (HEADS * HD, D), D ** -0.5, 0.109375, ((0, 4),))
    return dict(vae_in=vae_in, vae_gain=vae_gain, w_conv=w_conv, b_conv=b_conv, w_lat=w_lat, b_lat=b_lat, w_emb=w_emb, b_emb=b_emb, clip_lengths=clip_lengths, clip_owner=clip_owner, clip_mod=clip_mod, w_qkv=w_qkv, w_out=w_out)


NEG = -1e+30

def frame_tables(clip_lengths, clip_owner, frames):
    count = clip_lengths.shape[0]
    ends = jnp.cumsum(clip_lengths).astype(jnp.int32)
    starts = (ends - clip_lengths).astype(jnp.int32)
    frame_ids = jnp.arange(frames, dtype=jnp.int32)
    inside = (frame_ids[:, None] >= starts[None, :]) & (frame_ids[:, None] < ends[None, :])
    inside_int = inside.astype(jnp.int32)
    live = lax.optimization_barrier(jnp.sum(inside_int, axis=1)) > 0
    clip_ids = jnp.arange(count, dtype=jnp.int32)
    same_owner = clip_owner[:, None] == clip_owner[None, :]
    earlier = clip_ids[:, None] > clip_ids[None, :]
    offset = lax.optimization_barrier(jnp.sum(jnp.where(same_owner & earlier, clip_lengths[None, :], 0), axis=1)).astype(jnp.int32)
    frame_clip = jnp.where(live, lax.optimization_barrier(jnp.sum(inside_int * clip_ids[None, :], axis=1)), -1).astype(jnp.int32)
    frame_owner = jnp.where(live, lax.optimization_barrier(jnp.sum(inside_int * clip_owner[None, :], axis=1)), -1).astype(jnp.int32)
    shifted = (offset - starts).astype(jnp.int32)
    frame_slot = jnp.where(live, lax.optimization_barrier(jnp.sum(inside_int * shifted[None, :], axis=1)) + frame_ids, -1).astype(jnp.int32)
    return (frame_clip, frame_owner, frame_slot)

def conv_section(vae_in, vae_gain, w_conv, b_conv, w_lat, b_lat, frame_clip):
    frames = vae_in.shape[0]
    values = vae_in.astype(jnp.float32)
    power = lax.optimization_barrier(jnp.mean(values * values, axis=-1, keepdims=True))
    act = jax.nn.silu(values * lax.rsqrt(power + 1e-06) * vae_gain.astype(jnp.float32)).astype(jnp.bfloat16)
    padded = jnp.pad(act, ((1, 1), (0, 0), (0, 0), (0, 0)))
    border = jnp.full((1,), -2, jnp.int32)
    clip_pad = jnp.concatenate([border, frame_clip, border])
    conv = jnp.zeros(values.shape, jnp.float32) + b_conv.astype(jnp.float32)
    for tap in range(3):
        keep = (clip_pad[tap:tap + frames] == frame_clip)[:, None, None, None]
        term = jnp.dot(padded[tap:tap + frames], w_conv[tap], preferred_element_type=jnp.float32)
        conv = conv + jnp.where(keep, term, 0.0)
    resid = (values + conv).astype(jnp.bfloat16)
    latent = jnp.dot(resid, w_lat, preferred_element_type=jnp.float32) + b_lat.astype(jnp.float32)
    rows = latent.shape[1]
    cols = latent.shape[2]
    latent = latent.reshape(frames, rows // 2, 2, cols // 2, 2, latent.shape[3])
    latent = latent.transpose(0, 1, 3, 2, 4, 5).reshape(frames, rows // 2, cols // 2, -1)
    return latent.astype(jnp.bfloat16)

def attend_group(x_group, slot_clip, clip_mod, w_qkv, w_out):
    frames, prow, pcol, width = x_group.shape
    tokg = frames * prow * pcol
    mods = jnp.take(clip_mod, jnp.maximum(slot_clip, 0), axis=0).astype(jnp.float32)
    values = x_group.astype(jnp.float32)
    mean = lax.optimization_barrier(jnp.mean(values, axis=-1, keepdims=True))
    centred = values - mean
    spread = lax.optimization_barrier(jnp.mean(centred * centred, axis=-1, keepdims=True))
    normed = centred * lax.rsqrt(spread + 1e-06)
    hidden = normed * (1.0 + mods[:, None, None, 1, :]) + mods[:, None, None, 0, :]
    hidden = hidden.astype(jnp.bfloat16).reshape(tokg, width)
    qkv = jnp.dot(hidden, w_qkv.reshape(width, 3 * width), preferred_element_type=jnp.float32).astype(jnp.bfloat16)
    qkv = qkv.reshape(tokg, 3, HEADS, HD)
    token_clip = jnp.repeat(slot_clip, prow * pcol, total_repeat_length=tokg)
    same = token_clip[:, None] == token_clip[None, :]

    def one_head(index):
        query = lax.dynamic_index_in_dim(qkv[:, 0], index, axis=1, keepdims=False)
        keys = lax.dynamic_index_in_dim(qkv[:, 1], index, axis=1, keepdims=False)
        vals = lax.dynamic_index_in_dim(qkv[:, 2], index, axis=1, keepdims=False)
        scores = jnp.dot(query, keys.T, preferred_element_type=jnp.float32) * HD ** (-0.5)
        masked = jnp.where(same, scores, NEG)
        top = lax.optimization_barrier(jnp.max(masked, axis=-1, keepdims=True))
        weights = jnp.exp(masked - top)
        probs = (weights / lax.optimization_barrier(jnp.sum(weights, axis=-1, keepdims=True))).astype(jnp.bfloat16)
        return jnp.dot(probs, vals, preferred_element_type=jnp.float32).astype(jnp.bfloat16)
    heads = lax.map(one_head, jnp.arange(HEADS, dtype=jnp.int32))
    attn = heads.transpose(1, 0, 2).reshape(tokg, width)
    proj = jnp.dot(attn, w_out, preferred_element_type=jnp.float32).reshape(frames, prow, pcol, width)
    out = values + mods[:, None, None, 2, :] * proj
    live = (slot_clip >= 0)[:, None, None, None]
    return jnp.where(live, out, 0.0).astype(jnp.bfloat16)

def reference(vae_in, vae_gain, w_conv, b_conv, w_lat, b_lat, w_emb, b_emb, clip_lengths, clip_owner, clip_mod, w_qkv, w_out):
    frames = vae_in.shape[0]
    groups = GROUPS
    group_frames = frames // groups
    frame_clip, frame_owner, frame_slot = frame_tables(clip_lengths, clip_owner, frames)
    patch = conv_section(vae_in, vae_gain, w_conv, b_conv, w_lat, b_lat, frame_clip)
    tokens = (jnp.dot(patch, w_emb, preferred_element_type=jnp.float32) + b_emb.astype(jnp.float32)).astype(jnp.bfloat16)
    group_ids = jnp.arange(groups, dtype=jnp.int32)
    slot_ids = jnp.arange(group_frames, dtype=jnp.int32)
    frame_ids = jnp.arange(frames, dtype=jnp.int32)
    match = (frame_owner[None, None, :] == group_ids[:, None, None]) & (frame_slot[None, None, :] == slot_ids[None, :, None])
    match_int = match.astype(jnp.int32)
    source = lax.optimization_barrier(jnp.sum(match_int * frame_ids, axis=-1)).astype(jnp.int32)
    valid = lax.optimization_barrier(jnp.sum(match_int, axis=-1)) > 0
    slot_clip = jnp.where(valid, lax.optimization_barrier(jnp.sum(match_int * frame_clip, axis=-1)), -1).astype(jnp.int32)
    gathered = jnp.take(tokens, source.reshape(-1), axis=0).reshape((groups, group_frames) + tokens.shape[1:])
    gathered = jnp.where(valid[:, :, None, None, None], gathered, jnp.zeros((), gathered.dtype))

    def run_group(pair):
        return attend_group(pair[0], pair[1], clip_mod, w_qkv, w_out)
    outs = lax.map(run_group, (gathered, slot_clip))
    return outs.reshape((groups * group_frames,) + tokens.shape[1:])
```

```python
import functools

import jax
import jax.numpy as jnp
from jax import lax
from jax.experimental import pallas as pl
from jax.experimental.pallas import tpu as pltpu
from jax.sharding import PartitionSpec as P

MESH = pl.DeviceIdType.MESH
F32 = jnp.float32
BF16 = jnp.bfloat16
D = 3072
QC = 768
LOG2E = 1.4426950408889634


def mm(a, b):
    return jnp.dot(a, b, preferred_element_type=F32)


def mm_t(a, b):
    return lax.dot_general(a, b, (((1,), (1,)), ((), ())), preferred_element_type=F32)


def iota(shape, dim):
    return lax.broadcasted_iota(jnp.int32, shape, dim)


def body(
    vae,
    gain,
    w_conv,
    b_conv,
    w_lat,
    b_lat,
    w_emb,
    b_emb,
    lengths,
    owner,
    mods,
    w_qkv,
    w_out,
    out,
    xin,
    act,
    wconv,
    ym,
    wemb,
    modv,
    wq,
    lhs,
    mqk,
    wown,
    wbuf,
    pbuf,
    precv,
    pk,
    mb,
    keysp,
    attn_int,
    attn_own,
    attn_blk,
    acc,
    ptf,
    loc_sem,
    halo_s,
    halo_r,
    zs_s,
    zs_r,
    p1_s,
    p1_r,
    p2_s,
    p2_r,
    fw_s,
    fw_r,
    sib_s,
    sib_r,
    aa_s,
    aa_r,
    mb_s,
    mb_r,
    pk_s,
    pk_r,
):
    c = lax.axis_index("clip")
    z = lax.axis_index("seq")
    core = lax.rem(c, 2)
    x = lax.rem(lax.div(c, 2), 4)
    y = lax.div(c, 8)

    def in_plane(dx, dy):
        return (lax.rem(y + dy + 4, 4) * 8 + lax.rem(x + dx + 4, 4) * 2 + core, z)

    sibling = (c + 1 - 2 * core, z)

    def remote(src, dst, ss, rs, dev):
        return pltpu.make_async_remote_copy(
            src_ref=src, dst_ref=dst, send_sem=ss, recv_sem=rs, device_id=dev, device_id_type=MESH
        )

    loads = {}

    def load(name, src, dst, k):
        loads[name] = pltpu.make_async_copy(src, dst, loc_sem.at[k])
        loads[name].start()

    load("vae", vae, xin.at[pl.ds(1, 16)], 0)
    load("wconv", w_conv, wconv, 1)
    load("wemb", w_emb, wemb, 2)
    load("mods", mods, modv, 3)
    for j in range(3):
        load(("wq", j), w_qkv.at[j], wq.at[j], 4 + j)
    for q in range(4):
        load(("wo", q), w_out.at[:, pl.ds(q * QC, QC)], wown.at[q], 7 + q)

    barrier = pltpu.get_barrier_semaphore()

    def greet(g, carry):
        @pl.when(g != c)
        def _():
            pl.semaphore_signal(barrier, inc=1, device_id=(g, z), device_id_type=MESH)

        return carry

    lax.fori_loop(0, 32, greet, 0)
    for r in range(1, 4):
        pl.semaphore_signal(
            barrier, inc=1, device_id=(c, lax.rem(z + r, 4)), device_id_type=MESH
        )
    pl.semaphore_wait(barrier, 34)

    nxt = (lax.rem(c + 1, 32), z)
    prv = (lax.rem(c + 31, 32), z)
    halo = [
        remote(vae.at[pl.ds(15, 1)], xin.at[pl.ds(0, 1)], halo_s.at[0], halo_r.at[0], nxt),
        remote(vae.at[pl.ds(0, 1)], xin.at[pl.ds(17, 1)], halo_s.at[1], halo_r.at[1], prv),
    ]
    for cp in halo:
        cp.start()

    quarter = [2 * core, 2 * core + 1]
    piece = [
        pl.multiple_of(y * 192 + x * 48, 16),
        pl.multiple_of(x * 192 + y * 48, 16),
    ]
    scatter = []
    for k in range(2):
        for r in range(1, 4):
            i = k * 3 + r - 1
            cp = remote(
                w_out.at[pl.ds(piece[k], 48), pl.ds(pl.multiple_of(quarter[k] * QC, QC), QC)],
                wbuf.at[r, quarter[k], pl.ds(piece[k], 48), :],
                zs_s.at[i],
                zs_r.at[i],
                (c, lax.rem(z - r + 4, 4)),
            )
            cp.start()
            scatter.append(cp)

    lane = iota((8, 128), 1)
    fzero = jnp.zeros((8, 128), jnp.int32)

    def table(i, carry):
        starts, lens, owners, total, p_own, s_a, s_b, l_a, l_b = carry
        n = lengths[i]
        o = owner[i]
        here = lane == i
        starts = jnp.where(here, total, starts)
        lens = jnp.where(here, n, lens)
        owners = jnp.where(here, o, owners)
        mine = (o == c).astype(jnp.int32)
        low = (i < 32).astype(jnp.int32)
        p_own = p_own + mine * low * i
        s_a = s_a + mine * low * total
        s_b = s_b + mine * (1 - low) * total
        l_a = l_a + mine * low * n
        l_b = l_b + mine * (1 - low) * n
        return starts, lens, owners, total + n, p_own, s_a, s_b, l_a, l_b

    i0 = jnp.int32(0)
    starts, lens, owners, total, p_own, s_a, s_b, l_a, l_b = lax.fori_loop(
        0, 64, table, (fzero - 1, fzero, fzero - 1, i0, i0, i0, i0, i0, i0)
    )
    starts = jnp.where(lane == 64, total, starts)
    p_own = jnp.minimum(p_own, 31)

    def activate(v):
        v = v.astype(F32)
        power = jnp.mean(v * v, axis=-1, keepdims=True)
        t = v * lax.rsqrt(power + 1e-06) * gain[...]
        return (t / (1.0 + jnp.exp(-t))).astype(BF16)

    loads["vae"].wait()

    def act_step(i, carry):
        act[pl.ds(1 + 2 * i, 2)] = activate(xin[pl.ds(1 + 2 * i, 2)])
        return carry

    lax.fori_loop(0, 8, act_step, 0)

    for cp in scatter:
        cp.wait_recv()
    phase1 = []
    for k in range(2):
        for n, d in enumerate((1, -1, 2)):
            i = k * 3 + n
            region = wbuf.at[pl.ds(1, 3), quarter[k], pl.ds(piece[k], 48), :]
            dev = in_plane(d, 0) if k == 0 else in_plane(0, d)
            cp = remote(region, region, p1_s.at[i], p1_r.at[i], dev)
            cp.start()
            phase1.append(cp)

    def wait_phase1():
        for k in range(2):
            for n, d in enumerate((1, -1, 2)):
                i = k * 3 + n
                if k == 0:
                    row = y * 192 + lax.rem(x - d + 4, 4) * 48
                else:
                    row = x * 192 + lax.rem(y - d + 4, 4) * 48
                region = wbuf.at[
                    pl.ds(1, 3), quarter[k], pl.ds(pl.multiple_of(row, 16), 48), :
                ]
                remote(region, region, p1_s.at[i], p1_r.at[i], sibling).wait_recv()

    for cp in halo:
        cp.wait_recv()
    act[pl.ds(0, 1)] = activate(xin[pl.ds(0, 1)])
    act[pl.ds(17, 1)] = activate(xin[pl.ds(17, 1)])

    loads["wconv"].wait()
    fid = c * 16 + iota((16, 128), 0)
    starts16 = jnp.concatenate([starts, starts], axis=0)
    lane16 = iota((16, 128), 1)
    begins = jnp.max(
        jnp.where((starts16 == fid) & (lane16 <= 64), 1.0, 0.0), axis=1, keepdims=True
    )
    ends = jnp.max(
        jnp.where((starts16 == fid + 1) & (lane16 <= 64), 1.0, 0.0), axis=1, keepdims=True
    )
    keep0 = jnp.broadcast_to(1.0 - begins, (16, 128))
    keep2 = jnp.broadcast_to(1.0 - ends, (16, 128))
    lat8 = jnp.concatenate([w_lat[...]] * 8, axis=0)
    blat8 = jnp.concatenate([b_lat[...]] * 8, axis=1)
    pos = iota((256, 128), 0)
    ln = iota((256, 128), 1)
    pos_key = ((pos & 31) >> 4) * 4 + ((pos >> 5) & 1) * 2 + (pos & 1)
    place_mask = pos_key == (ln >> 4)
    for i in range(4):
        f0 = 4 * i
        left = act[pl.ds(f0, 4)].reshape(256, 512)
        mid = act[pl.ds(f0 + 1, 4)].reshape(256, 512)
        right = act[pl.ds(f0 + 2, 4)].reshape(256, 512)

        def rows_of(col):
            return jnp.concatenate(
                [
                    jnp.broadcast_to(col[f0 + f : f0 + f + 1, 0:1], (64, 512))
                    for f in range(4)
                ],
                axis=0,
            )

        conv = b_conv[...] + mm(mid, wconv[1])
        conv = conv + rows_of(keep0) * mm(left, wconv[0])
        conv = conv + rows_of(keep2) * mm(right, wconv[2])
        resid = (xin[pl.ds(f0 + 1, 4)].reshape(256, 512).astype(F32) + conv).astype(BF16)
        lat = mm_t(resid, lat8) + blat8
        ym[pl.ds(256 * i, 256), :] = jnp.where(place_mask, lat, 0.0).astype(BF16)

    srow = iota((128, 1024), 0)
    scol = iota((128, 1024), 1)
    pick_pos = ((srow & 15) == (scol >> 6)) & ((srow >> 4) == ((scol >> 1) & 7))
    patches = mm(pick_pos.astype(F32).astype(BF16), ym[...])
    frame_rows = jnp.concatenate([patches[16 * j : 16 * j + 16] for j in range(8)], axis=1)
    halves = jnp.concatenate([frame_rows[:, :512], frame_rows[:, 512:]], axis=0).astype(BF16)

    def column(vec, sel):
        return jnp.sum(jnp.where(sel, vec, 0), axis=1, keepdims=True)

    g_row = iota((512, 128), 0) >> 4
    g_lane = iota((512, 128), 1)
    own512 = jnp.broadcast_to(owners[0:1], (512, 128)) == g_row
    st512 = jnp.broadcast_to(starts[0:1], (512, 128))
    ln512 = jnp.broadcast_to(lens[0:1], (512, 128))
    sel_a = own512 & (g_lane < 32)
    sel_b = own512 & (g_lane >= 32) & (g_lane < 64)
    ga_s, ga_l = column(st512, sel_a), column(ln512, sel_a)
    gb_s, gb_l = column(st512, sel_b), column(ln512, sel_b)
    prow = iota((512, 32), 0)
    pcol = iota((512, 32), 1)
    frame = c * 16 + (pcol & 15)
    at = prow & 7
    wanted = ((frame == ga_s + at) & (at < ga_l)) | ((frame == gb_s + at) & (at < gb_l))
    wanted = wanted & (((prow >> 3) & 1) == (pcol >> 4))
    pbuf[...] = mm(wanted.astype(F32).astype(BF16), halves).astype(BF16).reshape(32, 16, 512)

    def send_rows(g, carry):
        @pl.when(g != c)
        def _():
            remote(pbuf.at[g], precv.at[c], aa_s.at[g], aa_r.at[c], (g, z)).start()

        return carry

    lax.fori_loop(0, 32, send_rows, 0)
    precv[c] = pbuf[c]

    loads["wemb"].wait()
    loads["mods"].wait()
    we = wemb[...].astype(F32)
    we = we - jnp.mean(we, axis=1, keepdims=True)
    be = b_emb[...]
    be = be - jnp.mean(be, axis=1, keepdims=True)
    scale_a = 1.0 + modv[1, pl.ds(p_own, 1), :]
    scale_b = 1.0 + modv[1, pl.ds(p_own + 32, 1), :]
    shift_a = modv[0, pl.ds(p_own, 1), :]
    shift_b = modv[0, pl.ds(p_own + 32, 1), :]
    lhs[0:64] = (we * scale_a).astype(BF16)
    lhs[64:128] = (we * scale_b).astype(BF16)
    extra = jnp.concatenate(
        [be * scale_a, shift_a, be * scale_b, shift_b, jnp.zeros((12, D), F32)], axis=0
    )
    lhs[128:144] = extra.astype(BF16)
    full = jnp.concatenate([we, be, jnp.zeros((63, D), F32)], axis=0)
    hi = full.astype(BF16)
    lo = (full - hi.astype(F32)).astype(BF16)
    gram = (mm_t(hi, hi) + mm_t(hi, lo) + mm_t(lo, hi)) * (1.0 / D)
    gram_hi = gram.astype(BF16)
    gram_lo = (gram - gram_hi.astype(F32)).astype(BF16)

    bias_row = iota((80, 128), 0)
    bias_col = iota((80, 128), 1)
    for j in range(3):
        loads[("wq", j)].wait()
        prod = mm(lhs[...], wq[j]).astype(BF16)
        for k in range(2):
            part = jnp.concatenate([prod[64 * k : 64 * k + 64], prod[128:144]], axis=0)
            if j < 2:
                mqk[j, k] = part
            else:
                mb[0, k, 1, 0:80, :] = part
    for k in range(2):
        one = jnp.where((bias_row == 65 + 2 * k) & (bias_col == 68), 1.0, 0.0)
        for h in range(6):
            mq = mqk[0, k, :, 128 * h : 128 * h + 128]
            mk = jnp.concatenate(
                [mqk[1, k, :, 128 * h : 128 * h + 128], jnp.zeros((48, 128), BF16)], axis=0
            )
            bil = mm_t(mq, mk) * (LOG2E * 128 ** (-0.5)) + one
            mb[0, k, 0, 0:80, 128 * h : 128 * h + 128] = bil.astype(BF16)
    zero_rows = jnp.zeros((48, QC), BF16)
    for r in range(4):
        for k in range(2):
            for j in range(2):
                mb[r, k, j, 80:128, :] = zero_rows
    mb_send = []
    for r in range(1, 4):
        cp = remote(
            mb.at[0, :, :, pl.ds(0, 80), :],
            mb.at[r, :, :, pl.ds(0, 80), :],
            mb_s.at[r - 1],
            mb_r.at[r - 1],
            (c, lax.rem(z - r + 4, 4)),
        )
        cp.start()
        mb_send.append(cp)

    wait_phase1()
    line = [y, x]

    def block(k, d, half=None):
        row = lax.rem(line[k] + d + 4, 4) * 192
        size = 192
        if half is not None:
            row = row + half * 96
            size = 96
        return (pl.ds(1, 3), quarter[k], pl.ds(pl.multiple_of(row, 16), size), slice(None))

    def along(k, d):
        return in_plane(0, d) if k == 0 else in_plane(d, 0)

    sends = []

    def push(region, ss, rs, dev):
        cp = remote(wbuf.at[region], wbuf.at[region], ss, rs, dev)
        cp.start()
        sends.append(cp)

    def arrived(region, ss, rs):
        remote(wbuf.at[region], wbuf.at[region], ss, rs, sibling).wait_recv()

    for k in range(2):
        for n, d in enumerate((1, -1)):
            push(block(k, 0), p2_s.at[2 * k + n], p2_r.at[2 * k + n], along(k, d))
    for k in range(2):
        push(block(k, 0), sib_s.at[4 * k], sib_r.at[4 * k], sibling)

    def get_rows(s, carry):
        @pl.when(s != c)
        def _():
            remote(pbuf.at[s], precv.at[s], aa_s.at[s], aa_r.at[s], (s, z)).wait_recv()

        return carry

    lax.fori_loop(0, 32, get_rows, 0)
    krow = iota((32, 512), 0)
    kcol = iota((32, 512), 1)
    kj = krow & 7
    k_first = jnp.where(((krow >> 3) & 1) == 0, s_a, s_b)
    k_len = jnp.where(((krow >> 3) & 1) == 0, l_a, l_b)
    take = (
        (((k_first + kj) >> 4) == (kcol >> 4))
        & (kj == (kcol & 7))
        & ((krow >> 4) == ((kcol >> 3) & 1))
        & (kj < k_len)
    )
    pk[0] = mm(take.astype(F32).astype(BF16), precv[...].reshape(512, 512)).astype(BF16)
    pk_send = []
    for r in range(1, 4):
        cp = remote(
            pk.at[0], pk.at[r], pk_s.at[r - 1], pk_r.at[r - 1], (c, lax.rem(z - r + 4, 4))
        )
        cp.start()
        pk_send.append(cp)
    for cp in pk_send:
        cp.wait_recv()

    klane = iota((512, 128), 1)
    kpos = iota((512, 128), 0) & 7
    tokens = []
    for k in range(2):
        blocks = []
        for r in range(4):
            rows = pk[r].astype(F32)
            for half in range(2):
                for b in range(8):
                    lo_row = half * 16 + 8 * k
                    blocks.append(rows[lo_row : lo_row + 8, 64 * b : 64 * b + 64])
        pt = jnp.concatenate(blocks, axis=0)
        pt = jnp.concatenate([pt, jnp.zeros((512, 64), F32)], axis=1)
        tokens.append(pt[0:128].astype(BF16))
        aug = jnp.where(klane == 64, 1.0, pt)
        augb = aug.astype(BF16)
        quad = mm(augb, gram_hi) + mm(augb, gram_lo)
        var = jnp.sum(aug * quad, axis=1, keepdims=True)
        rstd = lax.rsqrt(jnp.maximum(var, 0.0) + 1e-06)
        length = l_a if k == 0 else l_b
        bias = jnp.where(kpos < length, 0.0, -1e30)
        full_row = pt * rstd
        full_row = jnp.where(klane == 64 + 2 * k, rstd, full_row)
        full_row = jnp.where(klane == 65 + 2 * k, 1.0, full_row)
        full_row = jnp.where(klane == 68, bias, full_row)
        keysp[k] = full_row.astype(BF16)

    trow = iota((256, 256), 0)
    tcol = iota((256, 256), 1)
    tj = tcol & 7
    second = tcol >> 7
    t_slot = jnp.where(second == 0, tj, tj + l_a)
    t_ok = tj < jnp.where(second == 0, l_a, l_b)
    t_patch = ((tcol >> 3) & 1) * 8 + ((tcol >> 4) & 7)
    perm = ((trow >> 4) == t_slot) & ((trow & 15) == t_patch) & t_ok
    perm = perm.astype(F32).astype(BF16)
    ptf[...] = mm(perm, jnp.concatenate(tokens, axis=0)).astype(BF16)

    def attend(r):
        def one_clip(k, carry):
            keys = keysp[k]
            queries = mm(keys[0:128], mb[r, k, 0]).astype(BF16)
            den_lane = 65 + 2 * k
            sel = iota((128, 128), 1) == den_lane
            for h in range(6):
                s = mm_t(queries[:, 128 * h : 128 * h + 128], keys)
                top = jnp.max(s, axis=1, keepdims=True)
                w = jnp.exp2(s - top).astype(BF16)
                rr = mm(w, keys)
                den = jnp.sum(jnp.where(sel, rr, 0.0), axis=1, keepdims=True)
                rn = (rr / den).astype(BF16)
                o = mm(rn, mb[r, k, 1, :, 128 * h : 128 * h + 128])
                attn_int[pl.ds(pl.multiple_of(128 * k, 128), 128), 128 * h : 128 * h + 128] = (
                    o.astype(BF16)
                )
            return carry

        lax.fori_loop(0, 2, one_clip, 0)
        return mm(perm, attn_int[...]).astype(BF16)

    attn_own[...] = attend(0)

    for k in range(2):
        for n, d in enumerate((1, -1)):
            arrived(block(k, -d), p2_s.at[2 * k + n], p2_r.at[2 * k + n])
            push(block(k, -d, n), fw_s.at[2 * k + n], fw_r.at[2 * k + n], along(k, d))
    for k in range(2):
        for n, d in enumerate((1, -1)):
            push(block(k, -d), sib_s.at[4 * k + 1 + n], sib_r.at[4 * k + 1 + n], sibling)

    for q in range(4):
        loads[("wo", q)].wait()
        acc[q] = mm(attn_own[...], wown[q])

    def foreign(r, carry):
        remote(
            mb.at[0, :, :, pl.ds(0, 80), :],
            mb.at[r, :, :, pl.ds(0, 80), :],
            mb_s.at[r - 1],
            mb_r.at[r - 1],
            sibling,
        ).wait_recv()
        at_r = attend(r)
        for b in range(4):
            attn_blk[r - 1, b] = at_r[:, 192 * b : 192 * b + 192]
        return carry

    lax.fori_loop(1, 4, foreign, 0)

    def project(q, blk):
        rows = pl.ds(pl.multiple_of(blk * 192, 16), 192)
        total = acc[q]
        for r in range(3):
            total = total + mm(attn_blk[r, blk], wbuf[r + 1, q, rows, :])
        acc[q] = total

    other = [2 - 2 * core, 3 - 2 * core]

    def from_sibling(k, d, i):
        row = lax.rem(line[k] + d + 4, 4) * 192
        region = (pl.ds(1, 3), other[k], pl.ds(pl.multiple_of(row, 16), 192), slice(None))
        arrived(region, sib_s.at[4 * k + i], sib_r.at[4 * k + i])

    def project_step(k, d, i):
        blk = lax.rem(line[k] + d + 4, 4)
        project(quarter[k], blk)
        from_sibling(k, d, i)
        project(other[k], blk)

    for k in range(2):
        project_step(k, 0, 0)
    for k in range(2):
        for n, d in enumerate((1, -1)):
            project_step(k, -d, 1 + n)
    for k in range(2):
        for n, d in enumerate((1, -1)):
            arrived(block(k, 2, n), fw_s.at[2 * k + n], fw_r.at[2 * k + n])
        push(block(k, 2), sib_s.at[4 * k + 3], sib_r.at[4 * k + 3], sibling)
    for k in range(2):
        project_step(k, 2, 3)

    orow = iota((256, QC), 0) >> 4
    in_a = orow < l_a
    live = orow < l_a + l_b
    for q in range(4):
        cols = slice(q * QC, q * QC + QC)
        res = mm(ptf[:, 0:64], wemb[:, cols]) + b_emb[:, cols]
        gate = jnp.where(
            in_a, modv[2, pl.ds(p_own, 1), cols], modv[2, pl.ds(p_own + 32, 1), cols]
        )
        out[:, cols] = jnp.where(live, res + gate * acc[q], 0.0).astype(BF16)

    for cp in halo + scatter + phase1 + mb_send + pk_send + sends:
        cp.wait_send()

    def done_rows(g, carry):
        @pl.when(g != c)
        def _():
            remote(pbuf.at[g], precv.at[c], aa_s.at[g], aa_r.at[c], (g, z)).wait_send()

        return carry

    lax.fori_loop(0, 32, done_rows, 0)


def shards(
    vae_in,
    vae_gain,
    w_conv,
    b_conv,
    w_lat,
    b_lat,
    w_emb,
    b_emb,
    clip_lengths,
    clip_owner,
    clip_mod,
    w_qkv,
    w_out,
):
    anyspec = pl.BlockSpec(memory_space=pl.ANY)
    vmem = pl.BlockSpec(memory_space=pltpu.VMEM)
    smem = pl.BlockSpec(memory_space=pltpu.SMEM)
    dma = pltpu.SemaphoreType.DMA
    out = pl.pallas_call(
        body,
        out_shape=jax.ShapeDtypeStruct((256, D), BF16),
        in_specs=[
            anyspec,
            vmem,
            anyspec,
            vmem,
            vmem,
            vmem,
            anyspec,
            vmem,
            smem,
            smem,
            anyspec,
            anyspec,
            anyspec,
        ],
        out_specs=vmem,
        scratch_shapes=[
            pltpu.VMEM((18, 64, 512), BF16),
            pltpu.VMEM((18, 64, 512), BF16),
            pltpu.VMEM((3, 512, 512), BF16),
            pltpu.VMEM((1024, 128), BF16),
            pltpu.VMEM((64, D), BF16),
            pltpu.VMEM((3, 64, D), F32),
            pltpu.VMEM((3, D, QC), BF16),
            pltpu.VMEM((144, D), BF16),
            pltpu.VMEM((2, 2, 80, QC), BF16),
            pltpu.VMEM((4, QC, QC), BF16),
            pltpu.VMEM((4, 4, QC, QC), BF16),
            pltpu.VMEM((32, 16, 512), BF16),
            pltpu.VMEM((32, 16, 512), BF16),
            pltpu.VMEM((4, 32, 512), BF16),
            pltpu.VMEM((4, 2, 2, 128, QC), BF16),
            pltpu.VMEM((2, 512, 128), BF16),
            pltpu.VMEM((256, QC), BF16),
            pltpu.VMEM((256, QC), BF16),
            pltpu.VMEM((3, 4, 256, 192), BF16),
            pltpu.VMEM((4, 256, QC), F32),
            pltpu.VMEM((256, 128), BF16),
            dma((11,)),
            dma((2,)),
            dma((2,)),
            dma((6,)),
            dma((6,)),
            dma((6,)),
            dma((6,)),
            dma((4,)),
            dma((4,)),
            dma((4,)),
            dma((4,)),
            dma((8,)),
            dma((8,)),
            dma((32,)),
            dma((32,)),
            dma((3,)),
            dma((3,)),
            dma((3,)),
            dma((3,)),
        ],
        compiler_params=pltpu.CompilerParams(
            collective_id=0, has_side_effects=True, vmem_limit_bytes=60 * 2**20
        ),
    )(
        vae_in.reshape(16, 64, 512),
        vae_gain.reshape(1, 512),
        w_conv,
        b_conv.reshape(1, 512),
        w_lat.T,
        b_lat.reshape(1, 16),
        w_emb,
        b_emb.reshape(1, D),
        clip_lengths,
        clip_owner,
        clip_mod.transpose(1, 0, 2),
        w_qkv.transpose(1, 0, 2),
        w_out,
    )
    return out.reshape(16, 1, 16, D)


def solution(mesh):
    in_specs = (
        P("clip", "seq", None, None),
        P(),
        P(),
        P(),
        P(),
        P(),
        P(),
        P(),
        P(),
        P(),
        P(),
        P(None, None, "seq"),
        P("seq", None),
    )
    out_specs = P("clip", "seq", None, None)
    return jax.shard_map(shards, mesh=mesh, in_specs=in_specs, out_specs=out_specs, check_vma=False)
```

```python
import functools

import jax
import jax.numpy as jnp
from jax import lax
from jax.experimental import pallas as pl
from jax.experimental.pallas import tpu as pltpu
from jax.sharding import PartitionSpec as P

MESH = pl.DeviceIdType.MESH
F32 = jnp.float32
BF16 = jnp.bfloat16
D = 3072
QC = 768
LOG2E = 1.4426950408889634


def mm(a, b):
    return jnp.dot(a, b, preferred_element_type=F32)


def mm_t(a, b):
    return lax.dot_general(a, b, (((1,), (1,)), ((), ())), preferred_element_type=F32)


def iota(shape, dim):
    return lax.broadcasted_iota(jnp.int32, shape, dim)


def body(
    vae,
    gain,
    w_conv,
    b_conv,
    w_lat,
    b_lat,
    w_emb,
    b_emb,
    lengths,
    owner,
    mods,
    w_qkv,
    w_out,
    out,
    xin,
    act,
    wconv,
    ym,
    wemb,
    modv,
    wq,
    lhs,
    mqk,
    wown,
    wbuf,
    pbuf,
    precv,
    pk,
    mb,
    keysp,
    keyst,
    attn_int,
    attn_own,
    attn_blk,
    acc,
    ptf,
    loc_sem,
    halo_s,
    halo_r,
    zs_s,
    zs_r,
    zf_s,
    zf_r,
    ra_s,
    ra_r,
    rb_s,
    rb_r,
    fa_s,
    fa_r,
    fb_s,
    fb_r,
    sib_s,
    sib_r,
    aa_s,
    aa_r,
    mb_s,
    mb_r,
    pk_s,
    pk_r,
):
    c = lax.axis_index("clip")
    z = lax.axis_index("seq")
    core = lax.rem(c, 2)
    x = lax.rem(lax.div(c, 2), 4)
    y = lax.div(c, 8)

    def in_plane(dx, dy):
        return (lax.rem(y + dy + 4, 4) * 8 + lax.rem(x + dx + 4, 4) * 2 + core, z)

    sibling = (c + 1 - 2 * core, z)

    def remote(src, dst, ss, rs, dev):
        return pltpu.make_async_remote_copy(
            src_ref=src, dst_ref=dst, send_sem=ss, recv_sem=rs, device_id=dev, device_id_type=MESH
        )

    loads = {}

    def load(name, src, dst, k):
        loads[name] = pltpu.make_async_copy(src, dst, loc_sem.at[k])
        loads[name].start()

    load("vae", vae, xin.at[pl.ds(1, 16)], 0)
    load("wconv", w_conv, wconv, 1)
    load("wemb", w_emb, wemb, 2)
    load("mods", mods, modv, 3)
    for j in range(3):
        load(("wq", j), w_qkv.at[j], wq.at[j], 4 + j)
    for q in range(4):
        load(("wo", q), w_out.at[:, pl.ds(q * QC, QC)], wown.at[q], 7 + q)

    barrier = pltpu.get_barrier_semaphore()

    def greet(g, carry):
        @pl.when(g != c)
        def _():
            pl.semaphore_signal(barrier, inc=1, device_id=(g, z), device_id_type=MESH)

        return carry

    lax.fori_loop(0, 32, greet, 0)
    for r in range(1, 4):
        pl.semaphore_signal(
            barrier, inc=1, device_id=(c, lax.rem(z + r, 4)), device_id_type=MESH
        )
    pl.semaphore_wait(barrier, 34)

    nxt = (lax.rem(c + 1, 32), z)
    prv = (lax.rem(c + 31, 32), z)
    halo = [
        remote(vae.at[pl.ds(15, 1)], xin.at[pl.ds(0, 1)], halo_s.at[0], halo_r.at[0], nxt),
        remote(vae.at[pl.ds(0, 1)], xin.at[pl.ds(17, 1)], halo_s.at[1], halo_r.at[1], prv),
    ]
    for cp in halo:
        cp.start()

    quarter = [2 * core, 2 * core + 1]
    other = [2 - 2 * core, 3 - 2 * core]
    line = [y, x]
    up = (c, lax.rem(z + 1, 4))
    down = (c, lax.rem(z + 3, 4))
    sends = []

    def rows_at(k, d, half=None):
        row = lax.rem(line[k] + d + 4, 4) * 192
        if half is None:
            return pl.ds(pl.multiple_of(row, 16), 192)
        return pl.ds(pl.multiple_of(row + half * 96, 16), 96)

    def start(cp):
        cp.start()
        sends.append(cp)

    def scatter(half):
        for k in range(2):
            src = w_out.at[rows_at(k, 0, half), pl.ds(pl.multiple_of(quarter[k] * QC, QC), QC)]
            for slot, dev in ((0, down), (1, up)):
                i = 4 * half + 2 * k + slot
                dst = wbuf.at[slot, quarter[k], rows_at(k, 0, half), :]
                start(remote(src, dst, zs_s.at[i], zs_r.at[i], dev))

    def scattered(half):
        for k in range(2):
            for slot in range(2):
                i = 4 * half + 2 * k + slot
                dst = wbuf.at[slot, quarter[k], rows_at(k, 0, half), :]
                remote(dst, dst, zs_s.at[i], zs_r.at[i], sibling).wait_recv()

    def along(k, d):
        return in_plane(0, d) if k == 0 else in_plane(d, 0)

    def pair(k, d, half, q=None):
        return wbuf.at[pl.ds(0, 2), quarter[k] if q is None else q, rows_at(k, d, half), :]

    def third(k, d, half=None, q=None):
        return wbuf.at[2, quarter[k] if q is None else q, rows_at(k, d, half), :]

    def ring_pair(half):
        for k in range(2):
            for n, d in enumerate((1, -1)):
                i = 4 * half + 2 * k + n
                ref = pair(k, 0, half)
                start(remote(ref, ref, ra_s.at[i], ra_r.at[i], along(k, d)))

    def ring_third():
        for k in range(2):
            for n, d in enumerate((1, -1)):
                i = 2 * k + n
                ref = third(k, 0)
                start(remote(ref, ref, rb_s.at[i], rb_r.at[i], along(k, d)))

    def seq_forward(half):
        for k in range(2):
            i = 2 * k + half
            src = wbuf.at[1 - half, quarter[k], rows_at(k, 0, half), :]
            dst = third(k, 0, half)
            start(remote(src, dst, zf_s.at[i], zf_r.at[i], up if half == 0 else down))

    def seq_forwarded():
        for k in range(2):
            for half in range(2):
                i = 2 * k + half
                ref = third(k, 0, half)
                remote(ref, ref, zf_s.at[i], zf_r.at[i], sibling).wait_recv()

    def forward_pair(half):
        for k in range(2):
            for n, d in enumerate((1, -1)):
                i = 4 * half + 2 * k + n
                ref = pair(k, -d, half)
                remote(ref, ref, ra_s.at[i], ra_r.at[i], sibling).wait_recv()
                ref = wbuf.at[n, quarter[k], rows_at(k, -d, half), :]
                start(remote(ref, ref, fa_s.at[i], fa_r.at[i], along(k, d)))
        for k in range(2):
            for n, d in enumerate((1, -1)):
                share(k, pair(k, -d, half), 2 + 3 * n + half)

    def forward_third():
        for k in range(2):
            for n, d in enumerate((1, -1)):
                i = 2 * k + n
                ref = third(k, -d)
                remote(ref, ref, rb_s.at[i], rb_r.at[i], sibling).wait_recv()
                ref = third(k, -d, n)
                start(remote(ref, ref, fb_s.at[i], fb_r.at[i], along(k, d)))
        for k in range(2):
            for n, d in enumerate((1, -1)):
                share(k, third(k, -d), 4 + 3 * n)

    def opposite_pair(half):
        for k in range(2):
            for n, d in enumerate((1, -1)):
                i = 4 * half + 2 * k + n
                ref = wbuf.at[n, quarter[k], rows_at(k, 2, half), :]
                remote(ref, ref, fa_s.at[i], fa_r.at[i], sibling).wait_recv()
            share(k, pair(k, 2, half), 9 + half)

    def opposite_third():
        for k in range(2):
            for n in range(2):
                i = 2 * k + n
                ref = third(k, 2, n)
                remote(ref, ref, fb_s.at[i], fb_r.at[i], sibling).wait_recv()
            share(k, third(k, 2), 11)

    def share(k, ref, i):
        start(remote(ref, ref, sib_s.at[12 * k + i], sib_r.at[12 * k + i], sibling))

    def shared(k, d):
        first = {0: (0, 1, 8), 1: (5, 6, 7), -1: (2, 3, 4), 2: (9, 10, 11)}[d]
        for n, i in enumerate(first):
            if n < 2:
                ref = pair(k, d, n, other[k])
            else:
                ref = third(k, d, None, other[k])
            remote(ref, ref, sib_s.at[12 * k + i], sib_r.at[12 * k + i], sibling).wait_recv()

    scatter(0)

    lane = iota((8, 128), 1)
    fzero = jnp.zeros((8, 128), jnp.int32)

    def table(i, carry):
        starts, lens, owners, total, p_own, s_a, s_b, l_a, l_b = carry
        n = lengths[i]
        o = owner[i]
        here = lane == i
        starts = jnp.where(here, total, starts)
        lens = jnp.where(here, n, lens)
        owners = jnp.where(here, o, owners)
        mine = (o == c).astype(jnp.int32)
        low = (i < 32).astype(jnp.int32)
        p_own = p_own + mine * low * i
        s_a = s_a + mine * low * total
        s_b = s_b + mine * (1 - low) * total
        l_a = l_a + mine * low * n
        l_b = l_b + mine * (1 - low) * n
        return starts, lens, owners, total + n, p_own, s_a, s_b, l_a, l_b

    i0 = jnp.int32(0)
    starts, lens, owners, total, p_own, s_a, s_b, l_a, l_b = lax.fori_loop(
        0, 64, table, (fzero - 1, fzero, fzero - 1, i0, i0, i0, i0, i0, i0)
    )
    starts = jnp.where(lane == 64, total, starts)
    p_own = jnp.minimum(p_own, 31)

    def activate(v):
        v = v.astype(F32)
        power = jnp.mean(v * v, axis=-1, keepdims=True)
        t = v * lax.rsqrt(power + 1e-06) * gain[...]
        return (t / (1.0 + jnp.exp(-t))).astype(BF16)

    loads["vae"].wait()

    def act_step(i, carry):
        act[pl.ds(1 + 2 * i, 2)] = activate(xin[pl.ds(1 + 2 * i, 2)])
        return carry

    lax.fori_loop(0, 8, act_step, 0)

    scatter(1)

    for cp in halo:
        cp.wait_recv()
    act[pl.ds(0, 1)] = activate(xin[pl.ds(0, 1)])
    act[pl.ds(17, 1)] = activate(xin[pl.ds(17, 1)])

    loads["wconv"].wait()
    fid = c * 16 + iota((16, 128), 0)
    starts16 = jnp.concatenate([starts, starts], axis=0)
    lane16 = iota((16, 128), 1)
    begins = jnp.max(
        jnp.where((starts16 == fid) & (lane16 <= 64), 1.0, 0.0), axis=1, keepdims=True
    )
    ends = jnp.max(
        jnp.where((starts16 == fid + 1) & (lane16 <= 64), 1.0, 0.0), axis=1, keepdims=True
    )
    keep0 = jnp.broadcast_to(1.0 - begins, (16, 128))
    keep2 = jnp.broadcast_to(1.0 - ends, (16, 128))
    lat8 = jnp.concatenate([w_lat[...]] * 8, axis=0)
    blat8 = jnp.concatenate([b_lat[...]] * 8, axis=1)
    pos = iota((256, 128), 0)
    ln = iota((256, 128), 1)
    pos_key = ((pos & 31) >> 4) * 4 + ((pos >> 5) & 1) * 2 + (pos & 1)
    place_mask = pos_key == (ln >> 4)
    for i in range(4):
        f0 = 4 * i
        left = act[pl.ds(f0, 4)].reshape(256, 512)
        mid = act[pl.ds(f0 + 1, 4)].reshape(256, 512)
        right = act[pl.ds(f0 + 2, 4)].reshape(256, 512)

        def rows_of(col):
            return jnp.concatenate(
                [
                    jnp.broadcast_to(col[f0 + f : f0 + f + 1, 0:1], (64, 512))
                    for f in range(4)
                ],
                axis=0,
            )

        conv = b_conv[...] + mm(mid, wconv[1])
        conv = conv + rows_of(keep0) * mm(left, wconv[0])
        conv = conv + rows_of(keep2) * mm(right, wconv[2])
        resid = (xin[pl.ds(f0 + 1, 4)].reshape(256, 512).astype(F32) + conv).astype(BF16)
        lat = mm_t(resid, lat8) + blat8
        ym[pl.ds(256 * i, 256), :] = jnp.where(place_mask, lat, 0.0).astype(BF16)

    srow = iota((128, 1024), 0)
    scol = iota((128, 1024), 1)
    pick_pos = ((srow & 15) == (scol >> 6)) & ((srow >> 4) == ((scol >> 1) & 7))
    patches = mm(pick_pos.astype(F32).astype(BF16), ym[...])
    frame_rows = jnp.concatenate([patches[16 * j : 16 * j + 16] for j in range(8)], axis=1)
    halves = jnp.concatenate([frame_rows[:, :512], frame_rows[:, 512:]], axis=0).astype(BF16)

    def column(vec, sel):
        return jnp.sum(jnp.where(sel, vec, 0), axis=1, keepdims=True)

    g_row = iota((512, 128), 0) >> 4
    g_lane = iota((512, 128), 1)
    own512 = jnp.broadcast_to(owners[0:1], (512, 128)) == g_row
    st512 = jnp.broadcast_to(starts[0:1], (512, 128))
    ln512 = jnp.broadcast_to(lens[0:1], (512, 128))
    sel_a = own512 & (g_lane < 32)
    sel_b = own512 & (g_lane >= 32) & (g_lane < 64)
    ga_s, ga_l = column(st512, sel_a), column(ln512, sel_a)
    gb_s, gb_l = column(st512, sel_b), column(ln512, sel_b)
    prow = iota((512, 32), 0)
    pcol = iota((512, 32), 1)
    frame = c * 16 + (pcol & 15)
    at = prow & 7
    wanted = ((frame == ga_s + at) & (at < ga_l)) | ((frame == gb_s + at) & (at < gb_l))
    wanted = wanted & (((prow >> 3) & 1) == (pcol >> 4))
    pbuf[...] = mm(wanted.astype(F32).astype(BF16), halves).astype(BF16).reshape(32, 16, 512)

    def send_rows(g, carry):
        @pl.when(g != c)
        def _():
            remote(pbuf.at[g], precv.at[c], aa_s.at[g], aa_r.at[c], (g, z)).start()

        return carry

    lax.fori_loop(0, 32, send_rows, 0)
    precv[c] = pbuf[c]

    scattered(0)
    ring_pair(0)
    seq_forward(0)
    for k in range(2):
        share(k, pair(k, 0, 0), 0)

    loads["wemb"].wait()
    loads["mods"].wait()
    we = wemb[...].astype(F32)
    we = we - jnp.mean(we, axis=1, keepdims=True)
    be = b_emb[...]
    be = be - jnp.mean(be, axis=1, keepdims=True)
    scale_a = 1.0 + modv[1, pl.ds(p_own, 1), :]
    scale_b = 1.0 + modv[1, pl.ds(p_own + 32, 1), :]
    shift_a = modv[0, pl.ds(p_own, 1), :]
    shift_b = modv[0, pl.ds(p_own + 32, 1), :]
    lhs[0:64] = (we * scale_a).astype(BF16)
    lhs[64:128] = (we * scale_b).astype(BF16)
    pad = jnp.zeros((14, D), F32)
    extra = jnp.concatenate(
        [be * scale_a, shift_a, pad, be * scale_b, shift_b, pad], axis=0
    )
    lhs[128:160] = extra.astype(BF16)
    full = jnp.concatenate([we, be, jnp.zeros((63, D), F32)], axis=0)
    hi = full.astype(BF16)
    lo = (full - hi.astype(F32)).astype(BF16)
    gram = (mm_t(hi, hi) + mm_t(hi, lo) + mm_t(lo, hi)) * (1.0 / D)
    gram_hi = gram.astype(BF16)
    gram_lo = (gram - gram_hi.astype(F32)).astype(BF16)

    bias_row = iota((80, 128), 0)
    bias_col = iota((80, 128), 1)
    for j in range(3):
        loads[("wq", j)].wait()
        prod = mm(lhs[...], wq[j]).astype(BF16)
        for k in range(2):
            part = jnp.concatenate(
                [prod[64 * k : 64 * k + 64], prod[128 + 16 * k : 144 + 16 * k]], axis=0
            )
            if j < 2:
                mqk[j, k] = part
            else:
                mb[0, k, 1, 0:80, :] = part
    one = jnp.where((bias_row == 65) & (bias_col == 66), 1.0, 0.0)
    for k in range(2):
        for h in range(6):
            mq = mqk[0, k, :, 128 * h : 128 * h + 128]
            mk = jnp.concatenate(
                [mqk[1, k, :, 128 * h : 128 * h + 128], jnp.zeros((48, 128), BF16)], axis=0
            )
            bil = mm_t(mq, mk) * (LOG2E * 128 ** (-0.5)) + one
            mb[0, k, 0, 0:80, 128 * h : 128 * h + 128] = bil.astype(BF16)
    zero_rows = jnp.zeros((48, QC), BF16)
    for r in range(4):
        for k in range(2):
            for j in range(2):
                mb[r, k, j, 80:128, :] = zero_rows
    mb_send = []
    for r in range(1, 4):
        cp = remote(
            mb.at[0, :, :, pl.ds(0, 80), :],
            mb.at[r, :, :, pl.ds(0, 80), :],
            mb_s.at[r - 1],
            mb_r.at[r - 1],
            (c, lax.rem(z - r + 4, 4)),
        )
        cp.start()
        mb_send.append(cp)

    scattered(1)
    ring_pair(1)
    seq_forward(1)
    for k in range(2):
        share(k, pair(k, 0, 1), 1)

    def get_rows(s, carry):
        @pl.when(s != c)
        def _():
            remote(pbuf.at[s], precv.at[s], aa_s.at[s], aa_r.at[s], (s, z)).wait_recv()

        return carry

    lax.fori_loop(0, 32, get_rows, 0)
    krow = iota((32, 512), 0)
    kcol = iota((32, 512), 1)
    kj = krow & 7
    k_first = jnp.where(((krow >> 3) & 1) == 0, s_a, s_b)
    k_len = jnp.where(((krow >> 3) & 1) == 0, l_a, l_b)
    take = (
        (((k_first + kj) >> 4) == (kcol >> 4))
        & (kj == (kcol & 7))
        & ((krow >> 4) == ((kcol >> 3) & 1))
        & (kj < k_len)
    )
    pk[0] = mm(take.astype(F32).astype(BF16), precv[...].reshape(512, 512)).astype(BF16)
    pk_send = []
    for r in range(1, 4):
        cp = remote(
            pk.at[0], pk.at[r], pk_s.at[r - 1], pk_r.at[r - 1], (c, lax.rem(z - r + 4, 4))
        )
        cp.start()
        pk_send.append(cp)
    seq_forwarded()
    ring_third()
    for k in range(2):
        share(k, third(k, 0), 8)
    for cp in pk_send:
        cp.wait_recv()

    klane = iota((512, 128), 1)
    kpos = iota((512, 128), 0) & 7
    tokens = []
    for k in range(2):
        blocks = []
        for r in range(4):
            rows = pk[r].astype(F32)
            for half in range(2):
                for b in range(8):
                    lo_row = half * 16 + 8 * k
                    blocks.append(rows[lo_row : lo_row + 8, 64 * b : 64 * b + 64])
        pt = jnp.concatenate(blocks, axis=0)
        pt = jnp.concatenate([pt, jnp.zeros((512, 64), F32)], axis=1)
        tokens.append(pt[0:128].astype(BF16))
        aug = jnp.where(klane == 64, 1.0, pt)
        augb = aug.astype(BF16)
        quad = mm(augb, gram_hi) + mm(augb, gram_lo)
        var = jnp.sum(aug * quad, axis=1, keepdims=True)
        rstd = lax.rsqrt(jnp.maximum(var, 0.0) + 1e-06)
        length = l_a if k == 0 else l_b
        bias = jnp.where(kpos < length, 0.0, -1e30)
        full_row = pt * rstd
        full_row = jnp.where(klane == 64, rstd, full_row)
        full_row = jnp.where(klane == 65, 1.0, full_row)
        full_row = jnp.where(klane == 66, bias, full_row)
        keysp[k] = full_row.astype(BF16)
        keyst[k] = full_row.T.astype(BF16)

    trow = iota((256, 256), 0)
    tcol = iota((256, 256), 1)
    tj = tcol & 7
    second = tcol >> 7
    t_slot = jnp.where(second == 0, tj, tj + l_a)
    t_ok = tj < jnp.where(second == 0, l_a, l_b)
    t_patch = ((tcol >> 3) & 1) * 8 + ((tcol >> 4) & 7)
    perm = ((trow >> 4) == t_slot) & ((trow & 15) == t_patch) & t_ok
    perm = perm.astype(F32).astype(BF16)
    ptf[...] = mm(perm, jnp.concatenate(tokens, axis=0)).astype(BF16)

    def attend(r):
        def one_clip(k, carry):
            keys = keysp[k]
            queries = mm(keys[0:128], mb[r, k, 0]).astype(BF16)
            for g in range(3):
                lanes = [256 * g, 256 * g + 128]
                q2 = jnp.concatenate([queries[:, a : a + 128] for a in lanes], axis=0)
                s = mm(q2, keyst[k])
                top = jnp.max(s, axis=1, keepdims=True)
                w = jnp.exp2(s - top).astype(BF16)
                rr = mm(w, keys)
                rn = (rr * (1.0 / rr[:, 65:66])).astype(BF16)
                for n, a in enumerate(lanes):
                    o = mm(rn[128 * n : 128 * n + 128], mb[r, k, 1, :, a : a + 128])
                    attn_int[pl.ds(pl.multiple_of(128 * k, 128), 128), a : a + 128] = o.astype(
                        BF16
                    )
            return carry

        lax.fori_loop(0, 2, one_clip, 0)
        return mm(perm, attn_int[...]).astype(BF16)

    attn_own[...] = attend(0)

    forward_pair(0)
    for q in range(4):
        loads[("wo", q)].wait()
        acc[q] = mm(attn_own[...], wown[q])
    forward_pair(1)

    def foreign(slot, carry):
        r = lax.rem(2 * slot, 3) + 1
        remote(
            mb.at[0, :, :, pl.ds(0, 80), :],
            mb.at[r, :, :, pl.ds(0, 80), :],
            mb_s.at[r - 1],
            mb_r.at[r - 1],
            sibling,
        ).wait_recv()
        at_r = attend(r)
        for b in range(4):
            attn_blk[slot, b] = at_r[:, 192 * b : 192 * b + 192]
        return carry

    lax.fori_loop(0, 2, foreign, 0)
    forward_third()
    lax.fori_loop(2, 3, foreign, 0)

    def project(q, blk):
        rows = pl.ds(pl.multiple_of(blk * 192, 16), 192)
        total = acc[q]
        for slot in range(3):
            total = total + mm(attn_blk[slot, blk], wbuf[slot, q, rows, :])
        acc[q] = total

    def project_step(k, d):
        blk = lax.rem(line[k] + d + 4, 4)
        project(quarter[k], blk)
        shared(k, d)
        project(other[k], blk)

    for k in range(2):
        project_step(k, 0)
    opposite_pair(0)
    for k in range(2):
        project_step(k, -1)
    opposite_pair(1)
    for k in range(2):
        project_step(k, 1)
    opposite_third()
    for k in range(2):
        project_step(k, 2)

    orow = iota((256, QC), 0) >> 4
    in_a = orow < l_a
    live = orow < l_a + l_b
    for q in range(4):
        cols = slice(q * QC, q * QC + QC)
        res = mm(ptf[:, 0:64], wemb[:, cols]) + b_emb[:, cols]
        gate = jnp.where(
            in_a, modv[2, pl.ds(p_own, 1), cols], modv[2, pl.ds(p_own + 32, 1), cols]
        )
        out[:, cols] = jnp.where(live, res + gate * acc[q], 0.0).astype(BF16)

    for cp in halo + mb_send + pk_send + sends:
        cp.wait_send()

    def done_rows(g, carry):
        @pl.when(g != c)
        def _():
            remote(pbuf.at[g], precv.at[c], aa_s.at[g], aa_r.at[c], (g, z)).wait_send()

        return carry

    lax.fori_loop(0, 32, done_rows, 0)


def shards(
    vae_in,
    vae_gain,
    w_conv,
    b_conv,
    w_lat,
    b_lat,
    w_emb,
    b_emb,
    clip_lengths,
    clip_owner,
    clip_mod,
    w_qkv,
    w_out,
):
    anyspec = pl.BlockSpec(memory_space=pl.ANY)
    vmem = pl.BlockSpec(memory_space=pltpu.VMEM)
    smem = pl.BlockSpec(memory_space=pltpu.SMEM)
    dma = pltpu.SemaphoreType.DMA
    out = pl.pallas_call(
        body,
        out_shape=jax.ShapeDtypeStruct((256, D), BF16),
        in_specs=[
            anyspec,
            vmem,
            anyspec,
            vmem,
            vmem,
            vmem,
            anyspec,
            vmem,
            smem,
            smem,
            anyspec,
            anyspec,
            anyspec,
        ],
        out_specs=vmem,
        scratch_shapes=[
            pltpu.VMEM((18, 64, 512), BF16),
            pltpu.VMEM((18, 64, 512), BF16),
            pltpu.VMEM((3, 512, 512), BF16),
            pltpu.VMEM((1024, 128), BF16),
            pltpu.VMEM((64, D), BF16),
            pltpu.VMEM((3, 64, D), F32),
            pltpu.VMEM((3, D, QC), BF16),
            pltpu.VMEM((160, D), BF16),
            pltpu.VMEM((2, 2, 80, QC), BF16),
            pltpu.VMEM((4, QC, QC), BF16),
            pltpu.VMEM((3, 4, QC, QC), BF16),
            pltpu.VMEM((32, 16, 512), BF16),
            pltpu.VMEM((32, 16, 512), BF16),
            pltpu.VMEM((4, 32, 512), BF16),
            pltpu.VMEM((4, 2, 2, 128, QC), BF16),
            pltpu.VMEM((2, 512, 128), BF16),
            pltpu.VMEM((2, 128, 512), BF16),
            pltpu.VMEM((256, QC), BF16),
            pltpu.VMEM((256, QC), BF16),
            pltpu.VMEM((3, 4, 256, 192), BF16),
            pltpu.VMEM((4, 256, QC), F32),
            pltpu.VMEM((256, 128), BF16),
            dma((11,)),
            dma((2,)),
            dma((2,)),
            dma((8,)),
            dma((8,)),
            dma((4,)),
            dma((4,)),
            dma((8,)),
            dma((8,)),
            dma((4,)),
            dma((4,)),
            dma((8,)),
            dma((8,)),
            dma((4,)),
            dma((4,)),
            dma((24,)),
            dma((24,)),
            dma((32,)),
            dma((32,)),
            dma((3,)),
            dma((3,)),
            dma((3,)),
            dma((3,)),
        ],
        compiler_params=pltpu.CompilerParams(
            collective_id=0, has_side_effects=True, vmem_limit_bytes=60 * 2**20
        ),
    )(
        vae_in.reshape(16, 64, 512),
        vae_gain.reshape(1, 512),
        w_conv,
        b_conv.reshape(1, 512),
        w_lat.T,
        b_lat.reshape(1, 16),
        w_emb,
        b_emb.reshape(1, D),
        clip_lengths,
        clip_owner,
        clip_mod.transpose(1, 0, 2),
        w_qkv.transpose(1, 0, 2),
        w_out,
    )
    return out.reshape(16, 1, 16, D)


def solution(mesh):
    in_specs = (
        P("clip", "seq", None, None),
        P(),
        P(),
        P(),
        P(),
        P(),
        P(),
        P(),
        P(),
        P(),
        P(),
        P(None, None, "seq"),
        P("seq", None),
    )
    out_specs = P("clip", "seq", None, None)
    return jax.shard_map(shards, mesh=mesh, in_specs=in_specs, out_specs=out_specs, check_vma=False)
```

```python
import functools

import jax
import jax.numpy as jnp
from jax import lax
from jax.experimental import pallas as pl
from jax.experimental.pallas import tpu as pltpu
from jax.sharding import PartitionSpec as P

MESH = pl.DeviceIdType.MESH
F32 = jnp.float32
BF16 = jnp.bfloat16
D = 3072
QC = 768
LOG2E = 1.4426950408889634


def mm(a, b):
    return jnp.dot(a, b, preferred_element_type=F32)


def mm_t(a, b):
    return lax.dot_general(a, b, (((1,), (1,)), ((), ())), preferred_element_type=F32)


def iota(shape, dim):
    return lax.broadcasted_iota(jnp.int32, shape, dim)


def body(
    vae,
    gain,
    w_conv,
    b_conv,
    w_lat,
    b_lat,
    w_emb,
    b_emb,
    lengths,
    owner,
    mods,
    w_qkv,
    w_out,
    out,
    xin,
    act,
    wconv,
    ym,
    wemb,
    modv,
    wq,
    lhs,
    mqk,
    wown,
    wbuf,
    pbuf,
    precv,
    pk,
    mb,
    keysp,
    keyst,
    attn_int,
    attn_own,
    attn_blk,
    acc,
    ptf,
    loc_sem,
    halo_s,
    halo_r,
    zs_s,
    zs_r,
    zf_s,
    zf_r,
    ra_s,
    ra_r,
    rb_s,
    rb_r,
    fa_s,
    fa_r,
    fb_s,
    fb_r,
    sib_s,
    sib_r,
    aa_s,
    aa_r,
    mb_s,
    mb_r,
    pk_s,
    pk_r,
):
    c = lax.axis_index("clip")
    z = lax.axis_index("seq")
    core = lax.rem(c, 2)
    x = lax.rem(lax.div(c, 2), 4)
    y = lax.div(c, 8)

    def in_plane(dx, dy):
        return (lax.rem(y + dy + 4, 4) * 8 + lax.rem(x + dx + 4, 4) * 2 + core, z)

    sibling = (c + 1 - 2 * core, z)

    def remote(src, dst, ss, rs, dev):
        return pltpu.make_async_remote_copy(
            src_ref=src, dst_ref=dst, send_sem=ss, recv_sem=rs, device_id=dev, device_id_type=MESH
        )

    loads = {}

    def load(name, src, dst, k):
        loads[name] = pltpu.make_async_copy(src, dst, loc_sem.at[k])
        loads[name].start()

    load("vae", vae, xin.at[pl.ds(1, 16)], 0)
    load("wconv", w_conv, wconv, 1)
    load("wemb", w_emb, wemb, 2)
    load("mods", mods, modv, 3)
    for j in range(3):
        load(("wq", j), w_qkv.at[j], wq.at[j], 4 + j)
    for q in range(4):
        load(("wo", q), w_out.at[:, pl.ds(q * QC, QC)], wown.at[q], 7 + q)

    barrier = pltpu.get_barrier_semaphore()

    def greet(g, carry):
        @pl.when(g != c)
        def _():
            pl.semaphore_signal(barrier, inc=1, device_id=(g, z), device_id_type=MESH)

        return carry

    lax.fori_loop(0, 32, greet, 0)
    for r in range(1, 4):
        pl.semaphore_signal(
            barrier, inc=1, device_id=(c, lax.rem(z + r, 4)), device_id_type=MESH
        )
    pl.semaphore_wait(barrier, 34)

    nxt = (lax.rem(c + 1, 32), z)
    prv = (lax.rem(c + 31, 32), z)
    halo = [
        remote(vae.at[pl.ds(15, 1)], xin.at[pl.ds(0, 1)], halo_s.at[0], halo_r.at[0], nxt),
        remote(vae.at[pl.ds(0, 1)], xin.at[pl.ds(17, 1)], halo_s.at[1], halo_r.at[1], prv),
    ]
    for cp in halo:
        cp.start()

    quarter = [2 * core, 2 * core + 1]
    other = [2 - 2 * core, 3 - 2 * core]
    line = [y, x]
    up = (c, lax.rem(z + 1, 4))
    down = (c, lax.rem(z + 3, 4))
    sends = []

    def rows_at(k, d, half=None):
        row = lax.rem(line[k] + d + 4, 4) * 192
        if half is None:
            return pl.ds(pl.multiple_of(row, 16), 192)
        return pl.ds(pl.multiple_of(row + half * 96, 16), 96)

    def start(cp):
        cp.start()
        sends.append(cp)

    def scatter(half):
        for k in range(2):
            src = w_out.at[rows_at(k, 0, half), pl.ds(pl.multiple_of(quarter[k] * QC, QC), QC)]
            for slot, dev in ((0, down), (1, up)):
                i = 4 * half + 2 * k + slot
                dst = wbuf.at[slot, quarter[k], rows_at(k, 0, half), :]
                start(remote(src, dst, zs_s.at[i], zs_r.at[i], dev))

    def scattered(half):
        for k in range(2):
            for slot in range(2):
                i = 4 * half + 2 * k + slot
                dst = wbuf.at[slot, quarter[k], rows_at(k, 0, half), :]
                remote(dst, dst, zs_s.at[i], zs_r.at[i], sibling).wait_recv()

    def along(k, d):
        return in_plane(0, d) if k == 0 else in_plane(d, 0)

    def pair(k, d, half, q=None):
        return wbuf.at[pl.ds(0, 2), quarter[k] if q is None else q, rows_at(k, d, half), :]

    def third(k, d, half=None, q=None):
        return wbuf.at[2, quarter[k] if q is None else q, rows_at(k, d, half), :]

    def ring_pair(half):
        for k in range(2):
            for n, d in enumerate((1, -1)):
                i = 4 * half + 2 * k + n
                ref = pair(k, 0, half)
                start(remote(ref, ref, ra_s.at[i], ra_r.at[i], along(k, d)))

    def ring_third():
        for k in range(2):
            for n, d in enumerate((1, -1)):
                i = 2 * k + n
                ref = third(k, 0)
                start(remote(ref, ref, rb_s.at[i], rb_r.at[i], along(k, d)))

    def seq_forward(half):
        for k in range(2):
            i = 2 * k + half
            src = wbuf.at[1 - half, quarter[k], rows_at(k, 0, half), :]
            dst = third(k, 0, half)
            start(remote(src, dst, zf_s.at[i], zf_r.at[i], up if half == 0 else down))

    def seq_forwarded():
        for k in range(2):
            for half in range(2):
                i = 2 * k + half
                ref = third(k, 0, half)
                remote(ref, ref, zf_s.at[i], zf_r.at[i], sibling).wait_recv()

    def forward_pair(half):
        for k in range(2):
            for n, d in enumerate((1, -1)):
                i = 4 * half + 2 * k + n
                ref = pair(k, -d, half)
                remote(ref, ref, ra_s.at[i], ra_r.at[i], sibling).wait_recv()
                ref = wbuf.at[n, quarter[k], rows_at(k, -d, half), :]
                start(remote(ref, ref, fa_s.at[i], fa_r.at[i], along(k, d)))
        for k in range(2):
            for n, d in enumerate((1, -1)):
                share(k, pair(k, -d, half), 2 + 3 * n + half)

    def forward_third():
        for k in range(2):
            for n, d in enumerate((1, -1)):
                i = 2 * k + n
                ref = third(k, -d)
                remote(ref, ref, rb_s.at[i], rb_r.at[i], sibling).wait_recv()
                ref = third(k, -d, n)
                start(remote(ref, ref, fb_s.at[i], fb_r.at[i], along(k, d)))
        for k in range(2):
            for n, d in enumerate((1, -1)):
                share(k, third(k, -d), 4 + 3 * n)

    def opposite_pair(half):
        for k in range(2):
            for n, d in enumerate((1, -1)):
                i = 4 * half + 2 * k + n
                ref = wbuf.at[n, quarter[k], rows_at(k, 2, half), :]
                remote(ref, ref, fa_s.at[i], fa_r.at[i], sibling).wait_recv()
            share(k, pair(k, 2, half), 9 + half)

    def opposite_third():
        for k in range(2):
            for n in range(2):
                i = 2 * k + n
                ref = third(k, 2, n)
                remote(ref, ref, fb_s.at[i], fb_r.at[i], sibling).wait_recv()
            share(k, third(k, 2), 11)

    def share(k, ref, i):
        start(remote(ref, ref, sib_s.at[12 * k + i], sib_r.at[12 * k + i], sibling))

    def shared(k, d):
        first = {0: (0, 1, 8), 1: (5, 6, 7), -1: (2, 3, 4), 2: (9, 10, 11)}[d]
        for n, i in enumerate(first):
            if n < 2:
                ref = pair(k, d, n, other[k])
            else:
                ref = third(k, d, None, other[k])
            remote(ref, ref, sib_s.at[12 * k + i], sib_r.at[12 * k + i], sibling).wait_recv()

    scatter(0)

    lane = iota((8, 128), 1)
    fzero = jnp.zeros((8, 128), jnp.int32)

    def table(i, carry):
        starts, lens, owners, total, p_own, s_a, s_b, l_a, l_b = carry
        n = lengths[i]
        o = owner[i]
        here = lane == i
        starts = jnp.where(here, total, starts)
        lens = jnp.where(here, n, lens)
        owners = jnp.where(here, o, owners)
        mine = (o == c).astype(jnp.int32)
        low = (i < 32).astype(jnp.int32)
        p_own = p_own + mine * low * i
        s_a = s_a + mine * low * total
        s_b = s_b + mine * (1 - low) * total
        l_a = l_a + mine * low * n
        l_b = l_b + mine * (1 - low) * n
        return starts, lens, owners, total + n, p_own, s_a, s_b, l_a, l_b

    i0 = jnp.int32(0)
    starts, lens, owners, total, p_own, s_a, s_b, l_a, l_b = lax.fori_loop(
        0, 64, table, (fzero - 1, fzero, fzero - 1, i0, i0, i0, i0, i0, i0)
    )
    starts = jnp.where(lane == 64, total, starts)
    p_own = jnp.minimum(p_own, 31)

    def activate(v):
        v = v.astype(F32)
        power = jnp.mean(v * v, axis=-1, keepdims=True)
        t = v * lax.rsqrt(power + 1e-06) * gain[...]
        return (t / (1.0 + jnp.exp(-t))).astype(BF16)

    loads["vae"].wait()

    def act_step(i, carry):
        act[pl.ds(1 + 2 * i, 2)] = activate(xin[pl.ds(1 + 2 * i, 2)])
        return carry

    lax.fori_loop(0, 8, act_step, 0)

    scatter(1)

    for cp in halo:
        cp.wait_recv()
    act[pl.ds(0, 1)] = activate(xin[pl.ds(0, 1)])
    act[pl.ds(17, 1)] = activate(xin[pl.ds(17, 1)])

    loads["wconv"].wait()
    fid = c * 16 + iota((16, 128), 0)
    starts16 = jnp.concatenate([starts, starts], axis=0)
    lane16 = iota((16, 128), 1)
    begins = jnp.max(
        jnp.where((starts16 == fid) & (lane16 <= 64), 1.0, 0.0), axis=1, keepdims=True
    )
    ends = jnp.max(
        jnp.where((starts16 == fid + 1) & (lane16 <= 64), 1.0, 0.0), axis=1, keepdims=True
    )
    keep0 = jnp.broadcast_to(1.0 - begins, (16, 128))
    keep2 = jnp.broadcast_to(1.0 - ends, (16, 128))
    lat8 = jnp.concatenate([w_lat[...]] * 8, axis=0)
    blat8 = jnp.concatenate([b_lat[...]] * 8, axis=1)
    pos = iota((256, 128), 0)
    ln = iota((256, 128), 1)
    pos_key = ((pos & 31) >> 4) * 4 + ((pos >> 5) & 1) * 2 + (pos & 1)
    place_mask = pos_key == (ln >> 4)
    for i in range(4):
        f0 = 4 * i
        left = act[pl.ds(f0, 4)].reshape(256, 512)
        mid = act[pl.ds(f0 + 1, 4)].reshape(256, 512)
        right = act[pl.ds(f0 + 2, 4)].reshape(256, 512)

        def rows_of(col):
            return jnp.concatenate(
                [
                    jnp.broadcast_to(col[f0 + f : f0 + f + 1, 0:1], (64, 512))
                    for f in range(4)
                ],
                axis=0,
            )

        conv = b_conv[...] + mm(mid, wconv[1])
        conv = conv + rows_of(keep0) * mm(left, wconv[0])
        conv = conv + rows_of(keep2) * mm(right, wconv[2])
        resid = (xin[pl.ds(f0 + 1, 4)].reshape(256, 512).astype(F32) + conv).astype(BF16)
        lat = mm_t(resid, lat8) + blat8
        ym[pl.ds(256 * i, 256), :] = jnp.where(place_mask, lat, 0.0).astype(BF16)

    srow = iota((128, 1024), 0)
    scol = iota((128, 1024), 1)
    pick_pos = ((srow & 15) == (scol >> 6)) & ((srow >> 4) == ((scol >> 1) & 7))
    patches = mm(pick_pos.astype(F32).astype(BF16), ym[...])
    frame_rows = jnp.concatenate([patches[16 * j : 16 * j + 16] for j in range(8)], axis=1)
    halves = jnp.concatenate([frame_rows[:, :512], frame_rows[:, 512:]], axis=0).astype(BF16)

    def column(vec, sel):
        return jnp.sum(jnp.where(sel, vec, 0), axis=1, keepdims=True)

    g_row = iota((512, 128), 0) >> 4
    g_lane = iota((512, 128), 1)
    own512 = jnp.broadcast_to(owners[0:1], (512, 128)) == g_row
    st512 = jnp.broadcast_to(starts[0:1], (512, 128))
    ln512 = jnp.broadcast_to(lens[0:1], (512, 128))
    sel_a = own512 & (g_lane < 32)
    sel_b = own512 & (g_lane >= 32) & (g_lane < 64)
    ga_s, ga_l = column(st512, sel_a), column(ln512, sel_a)
    gb_s, gb_l = column(st512, sel_b), column(ln512, sel_b)
    prow = iota((512, 32), 0)
    pcol = iota((512, 32), 1)
    frame = c * 16 + (pcol & 15)
    at = prow & 7
    wanted = ((frame == ga_s + at) & (at < ga_l)) | ((frame == gb_s + at) & (at < gb_l))
    wanted = wanted & (((prow >> 3) & 1) == (pcol >> 4))
    pbuf[...] = mm(wanted.astype(F32).astype(BF16), halves).astype(BF16).reshape(32, 16, 512)

    def send_rows(g, carry):
        @pl.when(g != c)
        def _():
            remote(pbuf.at[g], precv.at[c], aa_s.at[g], aa_r.at[c], (g, z)).start()

        return carry

    lax.fori_loop(0, 32, send_rows, 0)
    precv[c] = pbuf[c]

    scattered(0)
    ring_pair(0)
    seq_forward(0)
    for k in range(2):
        share(k, pair(k, 0, 0), 0)

    loads["wemb"].wait()
    loads["mods"].wait()
    we = wemb[...].astype(F32)
    we = we - jnp.mean(we, axis=1, keepdims=True)
    be = b_emb[...]
    be = be - jnp.mean(be, axis=1, keepdims=True)
    scale_a = 1.0 + modv[1, pl.ds(p_own, 1), :]
    scale_b = 1.0 + modv[1, pl.ds(p_own + 32, 1), :]
    shift_a = modv[0, pl.ds(p_own, 1), :]
    shift_b = modv[0, pl.ds(p_own + 32, 1), :]
    lhs[0:64] = (we * scale_a).astype(BF16)
    lhs[64:128] = (we * scale_b).astype(BF16)
    extra = jnp.concatenate(
        [be * scale_a, shift_a, be * scale_b, shift_b, jnp.zeros((12, D), F32)], axis=0
    )
    lhs[128:144] = extra.astype(BF16)

    for j in range(3):
        loads[("wq", j)].wait()
        prod = mm(lhs[...], wq[j]).astype(BF16)
        if j < 2:
            mqk[j] = prod
        else:
            mb[0, :, 512:1280] = prod
    zero64 = jnp.zeros((64, 128), BF16)
    row128 = iota((128, 128), 0)
    scale = LOG2E * 128 ** (-0.5)
    extras = []
    for k in range(2):
        def part(j, h):
            cols = slice(128 * h, 128 * h + 128)
            return mqk[j, 64 * k : 64 * k + 64, cols]

        def side(h):
            return jnp.concatenate([part(0, h), mqk[0, 128:144, 128 * h : 128 * h + 128]], axis=0)

        pieces = []
        column_part = None
        for p in range(3):
            even = jnp.concatenate([part(1, 2 * p), zero64], axis=0)
            odd = jnp.concatenate([zero64, part(1, 2 * p + 1)], axis=0)
            pieces.append(mm_t(side(2 * p), even) + mm_t(side(2 * p + 1), odd))
        for h in range(6):
            key_bias = mqk[1, 128 + 2 * k : 129 + 2 * k, 128 * h : 128 * h + 128].astype(F32)
            spread = jnp.where(row128 == h, jnp.broadcast_to(key_bias, (128, 128)), 0.0)
            term = mm_t(side(h), spread.astype(BF16))
            column_part = term if column_part is None else column_part + term
        maps = jnp.concatenate(pieces + [column_part], axis=1) * scale
        mb[0, 64 * k : 64 * k + 64, 0:512] = maps[0:64].astype(BF16)
        extras.append(maps[64:80])
    mb[0, 128:144, 0:512] = jnp.where(iota((16, 512), 0) < 2, extras[0], extras[1]).astype(BF16)

    scattered(1)
    ring_pair(1)
    seq_forward(1)
    for k in range(2):
        share(k, pair(k, 0, 1), 1)

    def maps_copy(slot, dev):
        return remote(mb.at[0], mb.at[slot], mb_s.at[slot - 1], mb_r.at[slot - 1], dev)

    def maps_forward(slot, n, dev):
        rows = pl.ds(0, 80) if n == 0 else pl.ds(80, 64)
        src, dst = mb.at[slot, rows, :], mb.at[2, rows, :]
        return remote(src, dst, mb_s.at[3 + n], mb_r.at[3 + n], dev)

    start(maps_copy(1, down))
    start(maps_copy(3, up))

    def get_rows(s, carry):
        @pl.when(s != c)
        def _():
            remote(pbuf.at[s], precv.at[s], aa_s.at[s], aa_r.at[s], (s, z)).wait_recv()

        return carry

    lax.fori_loop(0, 32, get_rows, 0)
    krow = iota((32, 512), 0)
    kcol = iota((32, 512), 1)
    kj = krow & 7
    k_first = jnp.where(((krow >> 3) & 1) == 0, s_a, s_b)
    k_len = jnp.where(((krow >> 3) & 1) == 0, l_a, l_b)
    take = (
        (((k_first + kj) >> 4) == (kcol >> 4))
        & (kj == (kcol & 7))
        & ((krow >> 4) == ((kcol >> 3) & 1))
        & (kj < k_len)
    )
    pk[0] = mm(take.astype(F32).astype(BF16), precv[...].reshape(512, 512)).astype(BF16)
    pk_send = []
    for r in range(1, 4):
        cp = remote(
            pk.at[0], pk.at[r], pk_s.at[r - 1], pk_r.at[r - 1], (c, lax.rem(z - r + 4, 4))
        )
        cp.start()
        pk_send.append(cp)
    full = jnp.concatenate([we, be, jnp.zeros((63, D), F32)], axis=0)
    hi = full.astype(BF16)
    lo = (full - hi.astype(F32)).astype(BF16)
    gram = (mm_t(hi, hi) + mm_t(hi, lo) + mm_t(lo, hi)) * (1.0 / D)
    gram_hi = gram.astype(BF16)
    gram_lo = (gram - gram_hi.astype(F32)).astype(BF16)
    for cp in pk_send:
        cp.wait_recv()

    klane = iota((512, 128), 1)
    kpos = iota((512, 128), 0) & 7
    tokens = []
    for k in range(2):
        blocks = []
        for r in range(4):
            rows = pk[r].astype(F32)
            for half in range(2):
                for b in range(8):
                    lo_row = half * 16 + 8 * k
                    blocks.append(rows[lo_row : lo_row + 8, 64 * b : 64 * b + 64])
        pt = jnp.concatenate(blocks, axis=0)
        pt = jnp.concatenate([pt, jnp.zeros((512, 64), F32)], axis=1)
        tokens.append(pt[0:128].astype(BF16))
        aug = jnp.where(klane == 64, 1.0, pt)
        augb = aug.astype(BF16)
        quad = mm(augb, gram_hi) + mm(augb, gram_lo)
        var = jnp.sum(aug * quad, axis=1, keepdims=True)
        rstd = lax.rsqrt(jnp.maximum(var, 0.0) + 1e-06)
        length = l_a if k == 0 else l_b
        bias = jnp.where(kpos < length, 0.0, -1e30)
        full_row = pt * rstd
        full_row = jnp.where(klane == 64 + 2 * k, rstd, full_row)
        full_row = jnp.where(klane == 65 + 2 * k, 1.0, full_row)
        full_row = jnp.where(klane == 68, bias, full_row)
        keysp[k] = full_row.astype(BF16)
        keyst[k, 0] = full_row.T.astype(BF16)
        turned = jnp.concatenate([full_row[:, 64:128], full_row[:, 0:64]], axis=1)
        keyst[k, 1] = turned.T.astype(BF16)

    trow = iota((256, 256), 0)
    tcol = iota((256, 256), 1)
    tj = tcol & 7
    second = tcol >> 7
    t_slot = jnp.where(second == 0, tj, tj + l_a)
    t_ok = tj < jnp.where(second == 0, l_a, l_b)
    t_patch = ((tcol >> 3) & 1) * 8 + ((tcol >> 4) & 7)
    perm = ((trow >> 4) == t_slot) & ((trow & 15) == t_patch) & t_ok
    perm = perm.astype(F32).astype(BF16)
    ptf[...] = mm(perm, jnp.concatenate(tokens, axis=0)).astype(BF16)

    qlane = iota((128, 128), 1)
    tail = jnp.zeros((48, 1280), BF16)

    def attend(r):
        for k in range(2):
            keys = keysp[k]
            maps = jnp.concatenate([mb[r, 64 * k : 64 * k + 64], mb[r, 128:144], tail], axis=0)
            queries = mm(keys[0:128], maps[:, 0:512])
            for odd in range(2):
                main = (qlane < 64) if odd == 0 else (qlane >= 64)
                base = 64 - 64 * odd
                stack = []
                for p in range(3):
                    bias = queries[:, 384 + 2 * p + odd : 385 + 2 * p + odd]
                    rest = jnp.where(qlane == base + 2 * k, bias, 0.0)
                    rest = jnp.where(qlane == base + 4, 1.0, rest)
                    stack.append(jnp.where(main, queries[:, 128 * p : 128 * p + 128], rest))
                s = mm(jnp.concatenate(stack, axis=0).astype(BF16), keyst[k, odd])
                top = jnp.max(s, axis=1, keepdims=True)
                w = jnp.exp2(s - top).astype(BF16)
                rr = mm(w, keys)
                rn = (rr * (1.0 / rr[:, 65 + 2 * k : 66 + 2 * k])).astype(BF16)
                for p in range(3):
                    a = 128 * (2 * p + odd)
                    o = mm(rn[128 * p : 128 * p + 128], maps[:, 512 + a : 640 + a])
                    attn_int[128 * k : 128 * k + 128, a : a + 128] = o.astype(BF16)
        return mm(perm, attn_int[...]).astype(BF16)

    attn_own[...] = attend(0)

    forward_pair(0)
    for q in range(4):
        loads[("wo", q)].wait()
        acc[q] = mm(attn_own[...], wown[q])
    seq_forwarded()
    ring_third()
    for k in range(2):
        share(k, third(k, 0), 8)
    forward_pair(1)

    maps_copy(1, sibling).wait_recv()
    start(maps_forward(1, 1, down))
    maps_copy(3, sibling).wait_recv()
    start(maps_forward(3, 0, up))

    def foreign(slot, carry):
        at_r = attend(lax.rem(2 * slot, 3) + 1)
        for b in range(4):
            attn_blk[slot, b] = at_r[:, 192 * b : 192 * b + 192]
        return carry

    lax.fori_loop(0, 2, foreign, 0)
    forward_third()
    for n in range(2):
        maps_forward(1, n, sibling).wait_recv()
    lax.fori_loop(2, 3, foreign, 0)

    def project(q, blk):
        rows = pl.ds(pl.multiple_of(blk * 192, 16), 192)
        total = acc[q]
        for slot in range(3):
            total = total + mm(attn_blk[slot, blk], wbuf[slot, q, rows, :])
        acc[q] = total

    def project_step(k, d):
        blk = lax.rem(line[k] + d + 4, 4)
        project(quarter[k], blk)
        shared(k, d)
        project(other[k], blk)

    for k in range(2):
        project_step(k, 0)
    opposite_pair(0)
    for k in range(2):
        project_step(k, -1)
    opposite_pair(1)
    for k in range(2):
        project_step(k, 1)
    opposite_third()
    for k in range(2):
        project_step(k, 2)

    orow = iota((256, QC), 0) >> 4
    in_a = orow < l_a
    live = orow < l_a + l_b
    for q in range(4):
        cols = slice(q * QC, q * QC + QC)
        res = mm(ptf[:, 0:64], wemb[:, cols]) + b_emb[:, cols]
        gate = jnp.where(
            in_a, modv[2, pl.ds(p_own, 1), cols], modv[2, pl.ds(p_own + 32, 1), cols]
        )
        out[:, cols] = jnp.where(live, res + gate * acc[q], 0.0).astype(BF16)

    for cp in halo + pk_send + sends:
        cp.wait_send()

    def done_rows(g, carry):
        @pl.when(g != c)
        def _():
            remote(pbuf.at[g], precv.at[c], aa_s.at[g], aa_r.at[c], (g, z)).wait_send()

        return carry

    lax.fori_loop(0, 32, done_rows, 0)


def shards(
    vae_in,
    vae_gain,
    w_conv,
    b_conv,
    w_lat,
    b_lat,
    w_emb,
    b_emb,
    clip_lengths,
    clip_owner,
    clip_mod,
    w_qkv,
    w_out,
):
    anyspec = pl.BlockSpec(memory_space=pl.ANY)
    vmem = pl.BlockSpec(memory_space=pltpu.VMEM)
    smem = pl.BlockSpec(memory_space=pltpu.SMEM)
    dma = pltpu.SemaphoreType.DMA
    out = pl.pallas_call(
        body,
        out_shape=jax.ShapeDtypeStruct((256, D), BF16),
        in_specs=[
            anyspec,
            vmem,
            anyspec,
            vmem,
            vmem,
            vmem,
            anyspec,
            vmem,
            smem,
            smem,
            anyspec,
            anyspec,
            anyspec,
        ],
        out_specs=vmem,
        scratch_shapes=[
            pltpu.VMEM((18, 64, 512), BF16),
            pltpu.VMEM((18, 64, 512), BF16),
            pltpu.VMEM((3, 512, 512), BF16),
            pltpu.VMEM((1024, 128), BF16),
            pltpu.VMEM((64, D), BF16),
            pltpu.VMEM((3, 64, D), F32),
            pltpu.VMEM((3, D, QC), BF16),
            pltpu.VMEM((144, D), BF16),
            pltpu.VMEM((2, 144, QC), BF16),
            pltpu.VMEM((4, QC, QC), BF16),
            pltpu.VMEM((3, 4, QC, QC), BF16),
            pltpu.VMEM((32, 16, 512), BF16),
            pltpu.VMEM((32, 16, 512), BF16),
            pltpu.VMEM((4, 32, 512), BF16),
            pltpu.VMEM((4, 144, 1280), BF16),
            pltpu.VMEM((2, 512, 128), BF16),
            pltpu.VMEM((2, 2, 128, 512), BF16),
            pltpu.VMEM((256, QC), BF16),
            pltpu.VMEM((256, QC), BF16),
            pltpu.VMEM((3, 4, 256, 192), BF16),
            pltpu.VMEM((4, 256, QC), F32),
            pltpu.VMEM((256, 128), BF16),
            dma((11,)),
            dma((2,)),
            dma((2,)),
            dma((8,)),
            dma((8,)),
            dma((4,)),
            dma((4,)),
            dma((8,)),
            dma((8,)),
            dma((4,)),
            dma((4,)),
            dma((8,)),
            dma((8,)),
            dma((4,)),
            dma((4,)),
            dma((24,)),
            dma((24,)),
            dma((32,)),
            dma((32,)),
            dma((5,)),
            dma((5,)),
            dma((3,)),
            dma((3,)),
        ],
        compiler_params=pltpu.CompilerParams(
            collective_id=0, has_side_effects=True, vmem_limit_bytes=60 * 2**20
        ),
    )(
        vae_in.reshape(16, 64, 512),
        vae_gain.reshape(1, 512),
        w_conv,
        b_conv.reshape(1, 512),
        w_lat.T,
        b_lat.reshape(1, 16),
        w_emb,
        b_emb.reshape(1, D),
        clip_lengths,
        clip_owner,
        clip_mod.transpose(1, 0, 2),
        w_qkv.transpose(1, 0, 2),
        w_out,
    )
    return out.reshape(16, 1, 16, D)


def solution(mesh):
    in_specs = (
        P("clip", "seq", None, None),
        P(),
        P(),
        P(),
        P(),
        P(),
        P(),
        P(),
        P(),
        P(),
        P(),
        P(None, None, "seq"),
        P("seq", None),
    )
    out_specs = P("clip", "seq", None, None)
    return jax.shard_map(shards, mesh=mesh, in_specs=in_specs, out_specs=out_specs, check_vma=False)
```

```python
import functools

import jax
import jax.numpy as jnp
from jax import lax
from jax.experimental import pallas as pl
from jax.experimental.pallas import tpu as pltpu
from jax.sharding import PartitionSpec as P

MESH = pl.DeviceIdType.MESH
F32 = jnp.float32
BF16 = jnp.bfloat16
D = 3072
QC = 768
LOG2E = 1.4426950408889634


def mm(a, b):
    return jnp.dot(a, b, preferred_element_type=F32)


def mm_t(a, b):
    return lax.dot_general(a, b, (((1,), (1,)), ((), ())), preferred_element_type=F32)


def iota(shape, dim):
    return lax.broadcasted_iota(jnp.int32, shape, dim)


def body(
    vae,
    gain,
    w_conv,
    b_conv,
    w_lat,
    b_lat,
    w_emb,
    b_emb,
    lengths,
    owner,
    mods,
    w_qkv,
    w_out,
    out,
    xin,
    act,
    wconv,
    ym,
    wemb,
    modv,
    wq,
    lhs,
    mqk,
    wown,
    wbuf,
    pbuf,
    precv,
    pk,
    mb,
    keysp,
    keyst,
    attn_int,
    attn_own,
    attn_blk,
    acc,
    ptf,
    loc_sem,
    halo_s,
    halo_r,
    zs_s,
    zs_r,
    zf_s,
    zf_r,
    ra_s,
    ra_r,
    rb_s,
    rb_r,
    fa_s,
    fa_r,
    fb_s,
    fb_r,
    sib_s,
    sib_r,
    aa_s,
    aa_r,
    mb_s,
    mb_r,
    pk_s,
    pk_r,
):
    c = lax.axis_index("clip")
    z = lax.axis_index("seq")
    core = lax.rem(c, 2)
    x = lax.rem(lax.div(c, 2), 4)
    y = lax.div(c, 8)

    def in_plane(dx, dy):
        return (lax.rem(y + dy + 4, 4) * 8 + lax.rem(x + dx + 4, 4) * 2 + core, z)

    sibling = (c + 1 - 2 * core, z)

    def remote(src, dst, ss, rs, dev):
        return pltpu.make_async_remote_copy(
            src_ref=src, dst_ref=dst, send_sem=ss, recv_sem=rs, device_id=dev, device_id_type=MESH
        )

    loads = {}

    def load(name, src, dst, k):
        loads[name] = pltpu.make_async_copy(src, dst, loc_sem.at[k])
        loads[name].start()

    load("vae", vae, xin.at[pl.ds(1, 16)], 0)
    load("wconv", w_conv, wconv, 1)
    load("wemb", w_emb, wemb, 2)
    load("mods", mods, modv, 3)
    for j in range(3):
        load(("wq", j), w_qkv.at[j], wq.at[j], 4 + j)

    barrier = pltpu.get_barrier_semaphore()

    def greet(g, carry):
        @pl.when(g != c)
        def _():
            pl.semaphore_signal(barrier, inc=1, device_id=(g, z), device_id_type=MESH)

        return carry

    lax.fori_loop(0, 32, greet, 0)
    for r in range(1, 4):
        pl.semaphore_signal(
            barrier, inc=1, device_id=(c, lax.rem(z + r, 4)), device_id_type=MESH
        )

    quarter = [2 * core, 2 * core + 1]
    other = [2 - 2 * core, 3 - 2 * core]
    line = [y, x]
    up = (c, lax.rem(z + 1, 4))
    down = (c, lax.rem(z + 3, 4))
    sends = []

    def rows_at(k, d, half=None):
        row = lax.rem(line[k] + d + 4, 4) * 192
        if half is None:
            return pl.ds(pl.multiple_of(row, 16), 192)
        return pl.ds(pl.multiple_of(row + half * 96, 16), 96)

    def start(cp):
        cp.start()
        sends.append(cp)

    def scatter(half):
        for k in range(2):
            src = w_out.at[rows_at(k, 0, half), pl.ds(pl.multiple_of(quarter[k] * QC, QC), QC)]
            for slot, dev in ((0, down), (1, up)):
                i = 4 * half + 2 * k + slot
                dst = wbuf.at[slot, quarter[k], rows_at(k, 0, half), :]
                start(remote(src, dst, zs_s.at[i], zs_r.at[i], dev))

    def scattered(half):
        for k in range(2):
            for slot in range(2):
                i = 4 * half + 2 * k + slot
                dst = wbuf.at[slot, quarter[k], rows_at(k, 0, half), :]
                remote(dst, dst, zs_s.at[i], zs_r.at[i], sibling).wait_recv()

    def along(k, d):
        return in_plane(0, d) if k == 0 else in_plane(d, 0)

    def pair(k, d, half, q=None):
        return wbuf.at[pl.ds(0, 2), quarter[k] if q is None else q, rows_at(k, d, half), :]

    def third(k, d, half=None, q=None):
        return wbuf.at[2, quarter[k] if q is None else q, rows_at(k, d, half), :]

    def ring_pair(half):
        for k in range(2):
            for n, d in enumerate((1, -1)):
                i = 4 * half + 2 * k + n
                ref = pair(k, 0, half)
                start(remote(ref, ref, ra_s.at[i], ra_r.at[i], along(k, d)))

    def ring_third():
        for k in range(2):
            for n, d in enumerate((1, -1)):
                i = 2 * k + n
                ref = third(k, 0)
                start(remote(ref, ref, rb_s.at[i], rb_r.at[i], along(k, d)))

    def seq_forward(half):
        for k in range(2):
            i = 2 * k + half
            src = wbuf.at[1 - half, quarter[k], rows_at(k, 0, half), :]
            dst = third(k, 0, half)
            start(remote(src, dst, zf_s.at[i], zf_r.at[i], up if half == 0 else down))

    def seq_forwarded():
        for k in range(2):
            for half in range(2):
                i = 2 * k + half
                ref = third(k, 0, half)
                remote(ref, ref, zf_s.at[i], zf_r.at[i], sibling).wait_recv()

    def forward_pair(half):
        for k in range(2):
            for n, d in enumerate((1, -1)):
                i = 4 * half + 2 * k + n
                ref = pair(k, -d, half)
                remote(ref, ref, ra_s.at[i], ra_r.at[i], sibling).wait_recv()
                ref = wbuf.at[n, quarter[k], rows_at(k, -d, half), :]
                start(remote(ref, ref, fa_s.at[i], fa_r.at[i], along(k, d)))
        for k in range(2):
            for n, d in enumerate((1, -1)):
                share(k, pair(k, -d, half), 2 + 3 * n + half)

    def forward_third():
        for k in range(2):
            for n, d in enumerate((1, -1)):
                i = 2 * k + n
                ref = third(k, -d)
                remote(ref, ref, rb_s.at[i], rb_r.at[i], sibling).wait_recv()
                ref = third(k, -d, n)
                start(remote(ref, ref, fb_s.at[i], fb_r.at[i], along(k, d)))
        for k in range(2):
            for n, d in enumerate((1, -1)):
                share(k, third(k, -d), 4 + 3 * n)

    def opposite_pair(half):
        for k in range(2):
            for n, d in enumerate((1, -1)):
                i = 4 * half + 2 * k + n
                ref = wbuf.at[n, quarter[k], rows_at(k, 2, half), :]
                remote(ref, ref, fa_s.at[i], fa_r.at[i], sibling).wait_recv()
            share(k, pair(k, 2, half), 9 + half)

    def opposite_third():
        for k in range(2):
            for n in range(2):
                i = 2 * k + n
                ref = third(k, 2, n)
                remote(ref, ref, fb_s.at[i], fb_r.at[i], sibling).wait_recv()
            share(k, third(k, 2), 11)

    def share(k, ref, i):
        start(remote(ref, ref, sib_s.at[12 * k + i], sib_r.at[12 * k + i], sibling))

    def shared(k, d, slots):
        first = {0: (0, 1, 8), 1: (5, 6, 7), -1: (2, 3, 4), 2: (9, 10, 11)}[d]
        for n, i in enumerate(first):
            if (n == 2 and 2 not in slots) or (n < 2 and 0 not in slots):
                continue
            if n < 2:
                ref = pair(k, d, n, other[k])
            else:
                ref = third(k, d, None, other[k])
            remote(ref, ref, sib_s.at[12 * k + i], sib_r.at[12 * k + i], sibling).wait_recv()

    lane = iota((8, 128), 1)
    fzero = jnp.zeros((8, 128), jnp.int32)

    def table(i, carry):
        starts, lens, owners, total, p_own, s_a, s_b, l_a, l_b = carry
        n = lengths[i]
        o = owner[i]
        here = lane == i
        starts = jnp.where(here, total, starts)
        lens = jnp.where(here, n, lens)
        owners = jnp.where(here, o, owners)
        mine = (o == c).astype(jnp.int32)
        low = (i < 32).astype(jnp.int32)
        p_own = p_own + mine * low * i
        s_a = s_a + mine * low * total
        s_b = s_b + mine * (1 - low) * total
        l_a = l_a + mine * low * n
        l_b = l_b + mine * (1 - low) * n
        return starts, lens, owners, total + n, p_own, s_a, s_b, l_a, l_b

    i0 = jnp.int32(0)
    starts, lens, owners, total, p_own, s_a, s_b, l_a, l_b = lax.fori_loop(
        0, 64, table, (fzero - 1, fzero, fzero - 1, i0, i0, i0, i0, i0, i0)
    )
    starts = jnp.where(lane == 64, total, starts)
    p_own = jnp.minimum(p_own, 31)

    def activate(v):
        v = v.astype(F32)
        power = jnp.mean(v * v, axis=-1, keepdims=True)
        t = v * lax.rsqrt(power + 1e-06) * gain[...]
        return (t / (1.0 + jnp.exp(-t))).astype(BF16)

    loads["vae"].wait()

    def act_step(i, carry):
        act[pl.ds(1 + 2 * i, 2)] = activate(xin[pl.ds(1 + 2 * i, 2)])
        return carry

    lax.fori_loop(0, 8, act_step, 0)

    loads["wemb"].wait()
    loads["mods"].wait()
    we = wemb[...].astype(F32)
    we = we - jnp.mean(we, axis=1, keepdims=True)
    be = b_emb[...]
    be = be - jnp.mean(be, axis=1, keepdims=True)
    scale_a = 1.0 + modv[1, pl.ds(p_own, 1), :]
    scale_b = 1.0 + modv[1, pl.ds(p_own + 32, 1), :]
    shift_a = modv[0, pl.ds(p_own, 1), :]
    shift_b = modv[0, pl.ds(p_own + 32, 1), :]
    lhs[0:64] = (we * scale_a).astype(BF16)
    lhs[64:128] = (we * scale_b).astype(BF16)
    extra = jnp.concatenate(
        [be * scale_a, shift_a, be * scale_b, shift_b, jnp.zeros((12, D), F32)], axis=0
    )
    lhs[128:144] = extra.astype(BF16)

    pl.semaphore_wait(barrier, 34)

    nxt = (lax.rem(c + 1, 32), z)
    prv = (lax.rem(c + 31, 32), z)
    halo = [
        remote(vae.at[pl.ds(15, 1)], xin.at[pl.ds(0, 1)], halo_s.at[0], halo_r.at[0], nxt),
        remote(vae.at[pl.ds(0, 1)], xin.at[pl.ds(17, 1)], halo_s.at[1], halo_r.at[1], prv),
    ]
    for cp in halo:
        cp.start()

    scatter(0)

    for cp in halo:
        cp.wait_recv()
    act[pl.ds(0, 1)] = activate(xin[pl.ds(0, 1)])
    act[pl.ds(17, 1)] = activate(xin[pl.ds(17, 1)])

    scatter(1)
    for q in range(4):
        load(("wo", q), w_out.at[:, pl.ds(q * QC, QC)], wown.at[q], 7 + q)

    loads["wconv"].wait()
    fid = c * 16 + iota((16, 128), 0)
    starts16 = jnp.concatenate([starts, starts], axis=0)
    lane16 = iota((16, 128), 1)
    begins = jnp.max(
        jnp.where((starts16 == fid) & (lane16 <= 64), 1.0, 0.0), axis=1, keepdims=True
    )
    ends = jnp.max(
        jnp.where((starts16 == fid + 1) & (lane16 <= 64), 1.0, 0.0), axis=1, keepdims=True
    )
    keep0 = jnp.broadcast_to(1.0 - begins, (16, 128))
    keep2 = jnp.broadcast_to(1.0 - ends, (16, 128))
    lat8 = jnp.concatenate([w_lat[...]] * 8, axis=0)
    blat8 = jnp.concatenate([b_lat[...]] * 8, axis=1)
    pos = iota((256, 128), 0)
    ln = iota((256, 128), 1)
    pos_key = ((pos & 31) >> 4) * 4 + ((pos >> 5) & 1) * 2 + (pos & 1)
    place_mask = pos_key == (ln >> 4)
    for i in range(4):
        f0 = 4 * i
        left = act[pl.ds(f0, 4)].reshape(256, 512)
        mid = act[pl.ds(f0 + 1, 4)].reshape(256, 512)
        right = act[pl.ds(f0 + 2, 4)].reshape(256, 512)

        def rows_of(col):
            return jnp.concatenate(
                [
                    jnp.broadcast_to(col[f0 + f : f0 + f + 1, 0:1], (64, 512))
                    for f in range(4)
                ],
                axis=0,
            )

        conv = b_conv[...] + mm(mid, wconv[1])
        conv = conv + rows_of(keep0) * mm(left, wconv[0])
        conv = conv + rows_of(keep2) * mm(right, wconv[2])
        resid = (xin[pl.ds(f0 + 1, 4)].reshape(256, 512).astype(F32) + conv).astype(BF16)
        lat = mm_t(resid, lat8) + blat8
        ym[pl.ds(256 * i, 256), :] = jnp.where(place_mask, lat, 0.0).astype(BF16)

    srow = iota((128, 1024), 0)
    scol = iota((128, 1024), 1)
    pick_pos = ((srow & 15) == (scol >> 6)) & ((srow >> 4) == ((scol >> 1) & 7))
    patches = mm(pick_pos.astype(F32).astype(BF16), ym[...])
    frame_rows = jnp.concatenate([patches[16 * j : 16 * j + 16] for j in range(8)], axis=1)
    halves = jnp.concatenate([frame_rows[:, :512], frame_rows[:, 512:]], axis=0).astype(BF16)

    def column(vec, sel):
        return jnp.sum(jnp.where(sel, vec, 0), axis=1, keepdims=True)

    g_row = iota((512, 128), 0) >> 4
    g_lane = iota((512, 128), 1)
    own512 = jnp.broadcast_to(owners[0:1], (512, 128)) == g_row
    st512 = jnp.broadcast_to(starts[0:1], (512, 128))
    ln512 = jnp.broadcast_to(lens[0:1], (512, 128))
    sel_a = own512 & (g_lane < 32)
    sel_b = own512 & (g_lane >= 32) & (g_lane < 64)
    ga_s, ga_l = column(st512, sel_a), column(ln512, sel_a)
    gb_s, gb_l = column(st512, sel_b), column(ln512, sel_b)
    prow = iota((512, 32), 0)
    pcol = iota((512, 32), 1)
    frame = c * 16 + (pcol & 15)
    at = prow & 7
    wanted = ((frame == ga_s + at) & (at < ga_l)) | ((frame == gb_s + at) & (at < gb_l))
    wanted = wanted & (((prow >> 3) & 1) == (pcol >> 4))
    pbuf[...] = mm(wanted.astype(F32).astype(BF16), halves).astype(BF16).reshape(32, 16, 512)

    def send_rows(g, carry):
        @pl.when(g != c)
        def _():
            remote(pbuf.at[g], precv.at[c], aa_s.at[g], aa_r.at[c], (g, z)).start()

        return carry

    lax.fori_loop(0, 32, send_rows, 0)
    precv[c] = pbuf[c]

    for j in range(3):
        loads[("wq", j)].wait()
        prod = mm(lhs[...], wq[j]).astype(BF16)
        if j < 2:
            mqk[j] = prod
        else:
            mb[0, :, 512:1280] = prod
    zero64 = jnp.zeros((64, 128), BF16)
    row128 = iota((128, 128), 0)
    scale = LOG2E * 128 ** (-0.5)
    extras = []
    for k in range(2):
        def part(j, h):
            cols = slice(128 * h, 128 * h + 128)
            return mqk[j, 64 * k : 64 * k + 64, cols]

        def side(h):
            return jnp.concatenate([part(0, h), mqk[0, 128:144, 128 * h : 128 * h + 128]], axis=0)

        pieces = []
        column_part = None
        for p in range(3):
            even = jnp.concatenate([part(1, 2 * p), zero64], axis=0)
            odd = jnp.concatenate([zero64, part(1, 2 * p + 1)], axis=0)
            pieces.append(mm_t(side(2 * p), even) + mm_t(side(2 * p + 1), odd))
        for h in range(6):
            key_bias = mqk[1, 128 + 2 * k : 129 + 2 * k, 128 * h : 128 * h + 128].astype(F32)
            spread = jnp.where(row128 == h, jnp.broadcast_to(key_bias, (128, 128)), 0.0)
            term = mm_t(side(h), spread.astype(BF16))
            column_part = term if column_part is None else column_part + term
        maps = jnp.concatenate(pieces + [column_part], axis=1) * scale
        mb[0, 64 * k : 64 * k + 64, 0:512] = maps[0:64].astype(BF16)
        extras.append(maps[64:80])
    mb[0, 128:144, 0:512] = jnp.where(iota((16, 512), 0) < 2, extras[0], extras[1]).astype(BF16)

    scattered(0)
    ring_pair(0)
    seq_forward(0)
    for k in range(2):
        share(k, pair(k, 0, 0), 0)

    def maps_copy(slot, dev):
        return remote(mb.at[0], mb.at[slot], mb_s.at[slot - 1], mb_r.at[slot - 1], dev)

    def maps_forward(slot, n, dev):
        rows = pl.ds(0, 80) if n == 0 else pl.ds(80, 64)
        src, dst = mb.at[slot, rows, :], mb.at[2, rows, :]
        return remote(src, dst, mb_s.at[3 + n], mb_r.at[3 + n], dev)

    start(maps_copy(1, down))
    start(maps_copy(3, up))

    def get_rows(s, carry):
        @pl.when(s != c)
        def _():
            remote(pbuf.at[s], precv.at[s], aa_s.at[s], aa_r.at[s], (s, z)).wait_recv()

        return carry

    lax.fori_loop(0, 32, get_rows, 0)
    krow = iota((32, 512), 0)
    kcol = iota((32, 512), 1)
    kj = krow & 7
    k_first = jnp.where(((krow >> 3) & 1) == 0, s_a, s_b)
    k_len = jnp.where(((krow >> 3) & 1) == 0, l_a, l_b)
    take = (
        (((k_first + kj) >> 4) == (kcol >> 4))
        & (kj == (kcol & 7))
        & ((krow >> 4) == ((kcol >> 3) & 1))
        & (kj < k_len)
    )
    pk[0] = mm(take.astype(F32).astype(BF16), precv[...].reshape(512, 512)).astype(BF16)
    pk_send = []
    for r in range(1, 4):
        cp = remote(
            pk.at[0], pk.at[r], pk_s.at[r - 1], pk_r.at[r - 1], (c, lax.rem(z - r + 4, 4))
        )
        cp.start()
        pk_send.append(cp)
    scattered(1)
    ring_pair(1)
    seq_forward(1)
    for k in range(2):
        share(k, pair(k, 0, 1), 1)

    full = jnp.concatenate([we, be, jnp.zeros((63, D), F32)], axis=0)
    hi = full.astype(BF16)
    lo = (full - hi.astype(F32)).astype(BF16)
    gram = (mm_t(hi, hi) + mm_t(hi, lo) + mm_t(lo, hi)) * (1.0 / D)
    gram_hi = gram.astype(BF16)
    gram_lo = (gram - gram_hi.astype(F32)).astype(BF16)
    for cp in pk_send:
        cp.wait_recv()

    seq_forwarded()
    ring_third()
    for k in range(2):
        share(k, third(k, 0), 8)

    klane = iota((512, 128), 1)
    kpos = iota((512, 128), 0) & 7
    tokens = []
    for k in range(2):
        blocks = []
        for r in range(4):
            rows = pk[r].astype(F32)
            for half in range(2):
                for b in range(8):
                    lo_row = half * 16 + 8 * k
                    blocks.append(rows[lo_row : lo_row + 8, 64 * b : 64 * b + 64])
        pt = jnp.concatenate(blocks, axis=0)
        pt = jnp.concatenate([pt, jnp.zeros((512, 64), F32)], axis=1)
        tokens.append(pt[0:128].astype(BF16))
        aug = jnp.where(klane == 64, 1.0, pt)
        augb = aug.astype(BF16)
        quad = mm(augb, gram_hi) + mm(augb, gram_lo)
        var = jnp.sum(aug * quad, axis=1, keepdims=True)
        rstd = lax.rsqrt(jnp.maximum(var, 0.0) + 1e-06)
        length = l_a if k == 0 else l_b
        bias = jnp.where(kpos < length, 0.0, -1e30)
        full_row = pt * rstd
        full_row = jnp.where(klane == 64 + 2 * k, rstd, full_row)
        full_row = jnp.where(klane == 65 + 2 * k, 1.0, full_row)
        full_row = jnp.where(klane == 68, bias, full_row)
        keysp[k] = full_row.astype(BF16)
        keyst[k, 0] = full_row.T.astype(BF16)
        turned = jnp.concatenate([full_row[:, 64:128], full_row[:, 0:64]], axis=1)
        keyst[k, 1] = turned.T.astype(BF16)

    trow = iota((256, 256), 0)
    tcol = iota((256, 256), 1)
    tj = tcol & 7
    second = tcol >> 7
    t_slot = jnp.where(second == 0, tj, tj + l_a)
    t_ok = tj < jnp.where(second == 0, l_a, l_b)
    t_patch = ((tcol >> 3) & 1) * 8 + ((tcol >> 4) & 7)
    perm = ((trow >> 4) == t_slot) & ((trow & 15) == t_patch) & t_ok
    perm = perm.astype(F32).astype(BF16)
    ptf[...] = mm(perm, jnp.concatenate(tokens, axis=0)).astype(BF16)

    qlane = iota((128, 128), 1)
    tail = jnp.zeros((48, 1280), BF16)

    def attend(r):
        for k in range(2):
            keys = keysp[k]
            maps = jnp.concatenate([mb[r, 64 * k : 64 * k + 64], mb[r, 128:144], tail], axis=0)
            queries = mm(keys[0:128], maps[:, 0:512])
            for odd in range(2):
                main = (qlane < 64) if odd == 0 else (qlane >= 64)
                base = 64 - 64 * odd
                stack = []
                for p in range(3):
                    bias = queries[:, 384 + 2 * p + odd : 385 + 2 * p + odd]
                    rest = jnp.where(qlane == base + 2 * k, bias, 0.0)
                    rest = jnp.where(qlane == base + 4, 1.0, rest)
                    stack.append(jnp.where(main, queries[:, 128 * p : 128 * p + 128], rest))
                s = mm(jnp.concatenate(stack, axis=0).astype(BF16), keyst[k, odd])
                top = jnp.max(s, axis=1, keepdims=True)
                w = jnp.exp2(s - top).astype(BF16)
                rr = mm(w, keys)
                rn = (rr * (1.0 / rr[:, 65 + 2 * k : 66 + 2 * k])).astype(BF16)
                for p in range(3):
                    a = 128 * (2 * p + odd)
                    o = mm(rn[128 * p : 128 * p + 128], maps[:, 512 + a : 640 + a])
                    attn_int[128 * k : 128 * k + 128, a : a + 128] = o.astype(BF16)
        return mm(perm, attn_int[...]).astype(BF16)

    attn_own[...] = attend(0)

    forward_pair(0)
    for q in range(4):
        loads[("wo", q)].wait()
        acc[q] = mm(attn_own[...], wown[q])
    forward_pair(1)

    maps_copy(1, sibling).wait_recv()
    start(maps_forward(1, 1, down))
    maps_copy(3, sibling).wait_recv()
    start(maps_forward(3, 0, up))

    def foreign(slot, carry):
        at_r = attend(lax.rem(2 * slot, 3) + 1)
        for b in range(4):
            attn_blk[slot, b] = at_r[:, 192 * b : 192 * b + 192]
        return carry

    lax.fori_loop(0, 2, foreign, 0)

    def project(q, blk, slots):
        rows = pl.ds(pl.multiple_of(blk * 192, 16), 192)
        total = acc[q]
        for slot in slots:
            total = total + mm(attn_blk[slot, blk], wbuf[slot, q, rows, :])
        acc[q] = total

    def project_step(k, d, slots):
        blk = lax.rem(line[k] + d + 4, 4)
        project(quarter[k], blk, slots)
        shared(k, d, slots)
        project(other[k], blk, slots)

    for k in range(2):
        project_step(k, 0, (0, 1))
    forward_third()
    for n in range(2):
        maps_forward(1, n, sibling).wait_recv()
    lax.fori_loop(2, 3, foreign, 0)
    for k in range(2):
        project_step(k, 0, (2,))
    opposite_pair(0)
    opposite_pair(1)
    for d in (1, -1):
        for k in range(2):
            project_step(k, d, (0, 1, 2))
    opposite_third()
    for k in range(2):
        project_step(k, 2, (0, 1, 2))

    orow = iota((256, QC), 0) >> 4
    in_a = orow < l_a
    live = orow < l_a + l_b
    for q in range(4):
        cols = slice(q * QC, q * QC + QC)
        res = mm(ptf[:, 0:64], wemb[:, cols]) + b_emb[:, cols]
        gate = jnp.where(
            in_a, modv[2, pl.ds(p_own, 1), cols], modv[2, pl.ds(p_own + 32, 1), cols]
        )
        out[:, cols] = jnp.where(live, res + gate * acc[q], 0.0).astype(BF16)

    for cp in halo + pk_send + sends:
        cp.wait_send()

    def done_rows(g, carry):
        @pl.when(g != c)
        def _():
            remote(pbuf.at[g], precv.at[c], aa_s.at[g], aa_r.at[c], (g, z)).wait_send()

        return carry

    lax.fori_loop(0, 32, done_rows, 0)


def shards(
    vae_in,
    vae_gain,
    w_conv,
    b_conv,
    w_lat,
    b_lat,
    w_emb,
    b_emb,
    clip_lengths,
    clip_owner,
    clip_mod,
    w_qkv,
    w_out,
):
    anyspec = pl.BlockSpec(memory_space=pl.ANY)
    vmem = pl.BlockSpec(memory_space=pltpu.VMEM)
    smem = pl.BlockSpec(memory_space=pltpu.SMEM)
    dma = pltpu.SemaphoreType.DMA
    out = pl.pallas_call(
        body,
        out_shape=jax.ShapeDtypeStruct((256, D), BF16),
        in_specs=[
            anyspec,
            vmem,
            anyspec,
            vmem,
            vmem,
            vmem,
            anyspec,
            vmem,
            smem,
            smem,
            anyspec,
            anyspec,
            anyspec,
        ],
        out_specs=vmem,
        scratch_shapes=[
            pltpu.VMEM((18, 64, 512), BF16),
            pltpu.VMEM((18, 64, 512), BF16),
            pltpu.VMEM((3, 512, 512), BF16),
            pltpu.VMEM((1024, 128), BF16),
            pltpu.VMEM((64, D), BF16),
            pltpu.VMEM((3, 64, D), F32),
            pltpu.VMEM((3, D, QC), BF16),
            pltpu.VMEM((144, D), BF16),
            pltpu.VMEM((2, 144, QC), BF16),
            pltpu.VMEM((4, QC, QC), BF16),
            pltpu.VMEM((3, 4, QC, QC), BF16),
            pltpu.VMEM((32, 16, 512), BF16),
            pltpu.VMEM((32, 16, 512), BF16),
            pltpu.VMEM((4, 32, 512), BF16),
            pltpu.VMEM((4, 144, 1280), BF16),
            pltpu.VMEM((2, 512, 128), BF16),
            pltpu.VMEM((2, 2, 128, 512), BF16),
            pltpu.VMEM((256, QC), BF16),
            pltpu.VMEM((256, QC), BF16),
            pltpu.VMEM((3, 4, 256, 192), BF16),
            pltpu.VMEM((4, 256, QC), F32),
            pltpu.VMEM((256, 128), BF16),
            dma((11,)),
            dma((2,)),
            dma((2,)),
            dma((8,)),
            dma((8,)),
            dma((4,)),
            dma((4,)),
            dma((8,)),
            dma((8,)),
            dma((4,)),
            dma((4,)),
            dma((8,)),
            dma((8,)),
            dma((4,)),
            dma((4,)),
            dma((24,)),
            dma((24,)),
            dma((32,)),
            dma((32,)),
            dma((5,)),
            dma((5,)),
            dma((3,)),
            dma((3,)),
        ],
        compiler_params=pltpu.CompilerParams(
            collective_id=0, has_side_effects=True, vmem_limit_bytes=60 * 2**20
        ),
    )(
        vae_in.reshape(16, 64, 512),
        vae_gain.reshape(1, 512),
        w_conv,
        b_conv.reshape(1, 512),
        w_lat.T,
        b_lat.reshape(1, 16),
        w_emb,
        b_emb.reshape(1, D),
        clip_lengths,
        clip_owner,
        clip_mod.transpose(1, 0, 2),
        w_qkv.transpose(1, 0, 2),
        w_out,
    )
    return out.reshape(16, 1, 16, D)


def solution(mesh):
    in_specs = (
        P("clip", "seq", None, None),
        P(),
        P(),
        P(),
        P(),
        P(),
        P(),
        P(),
        P(),
        P(),
        P(),
        P(None, None, "seq"),
        P("seq", None),
    )
    out_specs = P("clip", "seq", None, None)
    return jax.shard_map(shards, mesh=mesh, in_specs=in_specs, out_specs=out_specs, check_vma=False)
```
